32 devices in a mesh: leaf: 8 (over z, y), rhs: 4 (over x, core).
Axes of the slice: x: 2, y: 2, z: 4, core: 2. Of those that a mesh axis runs over, the one named last changes fastest.
Arguments:
- right_sides: bfloat16 [512, 8192], P('rhs', 'leaf'), may hold values from -6 to 6
- block_order: int32 [64], replicated, may hold values from 0 to 63, each once
- leaf_basis: bfloat16 [8, 1024, 256], P('leaf'), may hold values from -0.1875 to 0.1875
- leaf_inner: bfloat16 [8, 256, 256], P('leaf'), may hold values from -0.375 to 0.375
- leaf_inverse: bfloat16 [8, 768, 768], P('leaf', 'rhs'), may hold values from -0.21875 to 0.21875
- leaf_coupling: bfloat16 [8, 768, 256], P('leaf'), may hold values from -0.21875 to 0.21875
- merge_one: bfloat16 [2048, 512], P('leaf'), may hold values from -0.25 to 0.25
- merge_two: bfloat16 [1024, 512], P('leaf'), may hold values from -0.25 to 0.25
- merge_three: bfloat16 [512, 512], P('leaf'), may hold values from -0.25 to 0.25
Outputs:
- leaf_part: bfloat16 [512, 6144], P('rhs', 'leaf')
- level_one: float32 [512, 1024], P('rhs', 'leaf')
- level_two: float32 [512, 512], P('rhs', 'leaf')
- level_three: float32 [512, 256], P('rhs', 'leaf')
- top_skeleton: float32 [512, 256], P('rhs', 'leaf')
The draws below stay inside these ranges and needn't reach their ends.
Inputs may be any that keep to these rules, and one draw needn't show every extreme that they name: block_order is a permutation: every block of the 64 appears exactly once.
All inputs are finite; a program needn't handle non-finite values.
Results may differ from the reference program's by a relative error of at most 0.007.
Values may be sent and summed in bfloat16 or wider, within the bound.
No kernel may reach another device: no remote copies, remote signals or barrier semaphores. Data moves between devices by JAX's collectives and lax.ppermute only.
A program may use at most 64 MiB of HBM per device.

```python
import jax
import jax.numpy as jnp
from jax import lax

M = 1024
R = 256
BLOCK = 128
E = 768
LEAVES = 8
NRHS = 512
N = 8192
NBLK = 64


def levels(rng, extent, cuts, least, largest):
    level, own = 1.0, jax.random.fold_in(rng, 6)
    for position, parts in cuts:
        heights = jnp.exp(jax.random.uniform(jax.random.fold_in(own, position), (parts,), jnp.float32, least / len(cuts), largest / len(cuts)))
        level = level * jnp.repeat(heights, extent[position] // parts).reshape([-1 if axis == position else 1 for axis in range(len(extent))])
    return level


def scatter_about(rng, extent, scale, most, split=(), dtype=jnp.bfloat16):
    result = jax.random.normal(rng, extent, jnp.float32) * scale
    if len(split) > 0:
        result = levels(rng, extent, split, -0.22, 0.18) * result
    return jnp.clip(result, min=-most, max=most).astype(dtype)


def setup_inputs(seed: int = 0) -> dict:
    seeds = jax.random.split(jax.random.key(seed), 10)
    right_sides = scatter_about(seeds[0], (NRHS, N), 1.0, 6.0, ((0, 4), (1, 8)))
    block_order = jax.random.permutation(seeds[1], NBLK).astype(jnp.int32)
    leaf_basis = scatter_about(seeds[2], (LEAVES, M, R), M ** -0.5, 0.1875, ((0, 8),))
    leaf_inner = scatter_about(seeds[3], (LEAVES, R, R), R ** -0.5, 0.375, ((0, 8),))
    leaf_inverse = scatter_about(seeds[4], (LEAVES, E, E), E ** -0.5, 0.21875, ((0, 8), (1, 4)))
    leaf_coupling = scatter_about(seeds[5], (LEAVES, E, R), E ** -0.5, 0.21875, ((0, 8),))
    merge_one = scatter_about(seeds[6], (LEAVES * R, 2 * R), (2 * R) ** -0.5, 0.25, ((0, 8),))
    merge_two = scatter_about(seeds[7], (LEAVES * R // 2, 2 * R), (2 * R) ** -0.5, 0.25, ((0, 8),))
    merge_three = scatter_about(seeds[8], (LEAVES * R // 4, 2 * R), (2 * R) ** -0.5, 0.25, ((0, 8),))
    return dict(right_sides=right_sides, block_order=block_order, leaf_basis=leaf_basis, leaf_inner=leaf_inner, leaf_inverse=leaf_inverse, leaf_coupling=leaf_coupling, merge_one=merge_one, merge_two=merge_two, merge_three=merge_three)


def reference(right_sides, block_order, leaf_basis, leaf_inner, leaf_inverse, leaf_coupling, merge_one, merge_two, merge_three):
    blocks = right_sides.reshape(NRHS, NBLK, BLOCK)
    tree_order = jnp.take(blocks, block_order.astype(jnp.int32), axis=1).reshape(NRHS, LEAVES, M)
    tree_order = jnp.transpose(tree_order, (1, 0, 2))

    def one_leaf(leaf_items):
        local_rows, basis_matrix, inner_matrix, inverse, coupling = leaf_items
        projected = jnp.dot(local_rows, basis_matrix, preferred_element_type=jnp.float32).astype(jnp.bfloat16)
        middle = jnp.dot(projected, inner_matrix, preferred_element_type=jnp.float32).astype(jnp.bfloat16)
        correction = jnp.dot(middle, basis_matrix.T, preferred_element_type=jnp.float32)
        reflected = (local_rows.astype(jnp.float32) - correction).astype(jnp.bfloat16)
        eliminated = jnp.dot(reflected[:, :E], inverse, preferred_element_type=jnp.float32).astype(jnp.bfloat16)
        skeleton = (reflected[:, E:].astype(jnp.float32) - jnp.dot(eliminated, coupling, preferred_element_type=jnp.float32)).astype(jnp.bfloat16)
        return eliminated, skeleton

    eliminated, skeleton = lax.map(one_leaf, (tree_order, leaf_basis, leaf_inner, leaf_inverse, leaf_coupling))
    leaf_part = jnp.transpose(eliminated, (1, 0, 2)).reshape(NRHS, LEAVES * E)
    current = jnp.transpose(skeleton, (1, 0, 2))
    outputs = []
    node_count = LEAVES
    upper_part = None
    for level_index, merge_table in enumerate((merge_one, merge_two, merge_three), start=1):
        node_count = node_count // 2
        group_count = 2 ** level_index
        paired = current.reshape(NRHS, node_count, 2 * R).astype(jnp.float32)
        operators = merge_table.reshape(node_count, 2 * R, 2 * R).astype(jnp.float32)
        joined = jnp.einsum("cpk,pkj->cpj", paired, operators)
        joined = joined.reshape(NRHS, node_count, group_count, 2, R // group_count)
        outputs.append(joined[:, :, :, 0, :].reshape(NRHS, node_count * R))
        upper_part = joined[:, :, :, 1, :].reshape(NRHS, node_count, R)
        current = upper_part.astype(jnp.bfloat16)
    return (leaf_part, outputs[0], outputs[1], outputs[2], upper_part.reshape(NRHS, node_count * R))
```

```python
import jax
import jax.numpy as jnp
from jax import lax
from jax.experimental import pallas as pl
from jax.experimental.pallas import tpu as pltpu
from jax.sharding import PartitionSpec as P

BLOCK = 128
NODE_LEAVES = 8


def partner_route(count, bit):
    return [(i, i ^ 1 << bit) for i in range(count) if i ^ 1 << bit < count]


def doubled(piece, axis, bit):
    upper = lax.axis_index(axis) >> bit & 1 == 1
    other = lax.ppermute(piece, axis, partner_route(lax.axis_size(axis), bit))
    first = jnp.where(upper, other, piece)
    second = jnp.where(upper, piece, other)
    return jnp.concatenate([first, second], axis=0)


def reorder_kernel(order_ref, rows_ref, out_ref):
    per_leaf = rows_ref.shape[2] // BLOCK
    for t in range(out_ref.shape[0] * per_leaf):
        source = order_ref[t]
        column = pl.multiple_of(lax.rem(source, per_leaf) * BLOCK, BLOCK)
        out_ref[t // per_leaf, :, pl.ds(t % per_leaf * BLOCK, BLOCK)] = rows_ref[
            lax.div(source, per_leaf), :, pl.ds(column, BLOCK)
        ]


def reorder(rows, block_order):
    leaf_count, per_group, row_count = rows.shape
    if per_group % 16 or leaf_count > 16:
        blocks = jnp.transpose(rows.reshape(leaf_count, per_group, -1, BLOCK), (0, 2, 1, 3))
        blocks = jnp.take(blocks.reshape(-1, per_group, BLOCK), block_order, axis=0)
        blocks = blocks.reshape(leaf_count, -1, per_group, BLOCK)
        return jnp.transpose(blocks, (0, 2, 1, 3)).reshape(leaf_count, per_group, row_count)
    return pl.pallas_call(
        reorder_kernel,
        out_shape=jax.ShapeDtypeStruct(rows.shape, rows.dtype),
        in_specs=[
            pl.BlockSpec(memory_space=pltpu.SMEM),
            pl.BlockSpec(memory_space=pltpu.VMEM),
        ],
        out_specs=pl.BlockSpec(memory_space=pltpu.VMEM),
    )(block_order, rows)


def shards(
    right_sides,
    block_order,
    leaf_basis,
    leaf_inner,
    leaf_inverse,
    leaf_coupling,
    merge_one,
    merge_two,
    merge_three,
):
    f32, bf16 = jnp.float32, jnp.bfloat16
    leaf_count = lax.axis_size("leaf")
    position = lax.axis_index("leaf")
    columns, row_count = right_sides.shape
    rank = merge_one.shape[0]

    inverse = leaf_inverse[0]
    for bit in reversed(range((lax.axis_size("rhs") - 1).bit_length())):
        upper = lax.axis_index("rhs") >> bit & 1 == 1
        other = lax.ppermute(inverse, "rhs", partner_route(lax.axis_size("rhs"), bit))
        first, second = jnp.where(upper, other, inverse), jnp.where(upper, inverse, other)
        span = leaf_inverse.shape[1]
        first = first.reshape(-1, 1, span, first.shape[1])
        second = second.reshape(-1, 1, span, second.shape[1])
        inverse = jnp.concatenate([first, second], axis=1).reshape(-1, first.shape[3])
    upper_rows = jnp.concatenate([merge_two, merge_three], axis=0)
    pair = lax.ppermute(upper_rows, "leaf", partner_route(leaf_count, 0))
    odd = position & 1 == 1
    low, high = jnp.where(odd, pair, upper_rows), jnp.where(odd, upper_rows, pair)
    cut = merge_two.shape[0]
    two_rows = jnp.concatenate([low[:cut], high[:cut]], axis=0)
    three_rows = doubled(jnp.concatenate([low[cut:], high[cut:]], axis=0), "leaf", 1)

    one_parts = merge_one.reshape(rank, 2, 2, rank // 2)
    one_eliminated = one_parts[:, :, 0].reshape(rank, rank)
    one_skeleton = one_parts[:, :, 1].reshape(rank, rank)
    through_two = lax.dot_general(
        two_rows, one_skeleton, (((0,), (1,)), ((), ())), preferred_element_type=f32
    ).astype(bf16)
    two_parts = through_two.reshape(4, 2, rank // 4, rank)
    through_three = lax.dot_general(
        three_rows,
        two_parts[:, 1].reshape(rank, rank),
        (((0,), (0,)), ((), ())),
        preferred_element_type=f32,
    ).astype(bf16)
    three_parts = through_three.reshape(NODE_LEAVES, rank // 4, rank)
    own_quad = position // 4 % 2
    two_eliminated = two_parts[:, 0]
    nothing = jnp.zeros_like(two_eliminated)
    two_spread = jnp.concatenate(
        [
            jnp.where(own_quad == 0, two_eliminated, nothing),
            jnp.where(own_quad == 1, two_eliminated, nothing),
        ],
        axis=0,
    )
    upper_table = jnp.concatenate([three_parts, two_spread], axis=1).reshape(-1, rank)

    outgoing = right_sides.reshape(leaf_count, columns // leaf_count, row_count)
    arrived = lax.all_to_all(outgoing, "leaf", split_axis=0, concat_axis=0, tiled=True)
    returning = reorder(arrived, block_order)
    placed = lax.all_to_all(returning, "leaf", split_axis=0, concat_axis=0, tiled=True).reshape(
        columns, row_count
    )

    basis = leaf_basis[0]
    projected = jnp.dot(placed, basis, preferred_element_type=f32).astype(bf16)
    middle = jnp.dot(projected, leaf_inner[0], preferred_element_type=f32).astype(bf16)
    correction = lax.dot_general(
        middle, basis, (((1,), (1,)), ((), ())), preferred_element_type=f32
    )
    reflected = (placed.astype(f32) - correction).astype(bf16)
    split_at = row_count - rank
    eliminated = jnp.dot(
        reflected[:, :split_at], inverse, preferred_element_type=f32
    ).astype(bf16)
    coupled = jnp.dot(eliminated, leaf_coupling[0], preferred_element_type=f32)
    skeleton = (reflected[:, split_at:].astype(f32) - coupled).astype(bf16)

    terms = lax.dot_general(
        upper_table, skeleton, (((1,), (1,)), ((), ())), preferred_element_type=f32
    ).astype(bf16)
    groups = None
    if leaf_count > NODE_LEAVES:
        groups = [
            list(range(i, i + NODE_LEAVES)) for i in range(0, leaf_count, NODE_LEAVES)
        ]
    received = lax.all_to_all(
        terms.reshape(NODE_LEAVES, -1, columns),
        "leaf",
        split_axis=0,
        concat_axis=0,
        tiled=True,
        axis_index_groups=groups,
    )
    one_terms = jnp.dot(skeleton, one_eliminated, preferred_element_type=f32)
    halves = one_terms[:, : rank // 2], one_terms[:, rank // 2 :]
    kept = jnp.where(odd, halves[1], halves[0])
    sent = jnp.where(odd, halves[0], halves[1])
    level_one = kept + lax.ppermute(sent, "leaf", partner_route(leaf_count, 0))
    total = jnp.sum(received.astype(f32), axis=0)
    eighth = rank // 8
    level_three = total[:eighth].T
    top_skeleton = total[eighth : 2 * eighth].T
    level_two = total[2 * eighth :].T
    return (eliminated, level_one, level_two, level_three, top_skeleton)


def solution(mesh):
    placed = (
        P("rhs", "leaf"),
        P(),
        P("leaf", None, None),
        P("leaf", None, None),
        P("leaf", "rhs", None),
        P("leaf", None, None),
        P("leaf", None),
        P("leaf", None),
        P("leaf", None),
    )
    return jax.shard_map(
        shards,
        mesh=mesh,
        in_specs=placed,
        out_specs=(P("rhs", "leaf"),) * 5,
        check_vma=False,
    )
```

```python
import jax
import jax.numpy as jnp
from jax import lax
from jax.experimental import pallas as pl
from jax.experimental.pallas import tpu as pltpu
from jax.sharding import PartitionSpec as P

BLOCK = 128
NODE_LEAVES = 8
INSIDE = pl.BlockSpec(memory_space=pltpu.VMEM)


def exchanged(piece, axis, flip):
    count = lax.axis_size(axis)
    return lax.ppermute(piece, axis, [(i, i ^ flip) for i in range(count) if i ^ flip < count])


def product(left, right, over=((1,), (0,))):
    return lax.dot_general(left, right, (over, ((), ())), preferred_element_type=jnp.float32)


def reorder_kernel(order_ref, rows_ref, out_ref):
    per_leaf = rows_ref.shape[2] // BLOCK
    for t in range(out_ref.shape[0] * per_leaf):
        source = order_ref[t]
        column = pl.multiple_of(lax.rem(source, per_leaf) * BLOCK, BLOCK)
        out_ref[t // per_leaf, :, pl.ds(t % per_leaf * BLOCK, BLOCK)] = rows_ref[
            lax.div(source, per_leaf), :, pl.ds(column, BLOCK)
        ]


def reorder(rows, block_order):
    leaf_count, per_group, row_count = rows.shape
    if per_group % 16 or leaf_count > 16:
        blocks = jnp.transpose(rows.reshape(leaf_count, per_group, -1, BLOCK), (0, 2, 1, 3))
        blocks = jnp.take(blocks.reshape(-1, per_group, BLOCK), block_order, axis=0)
        blocks = blocks.reshape(leaf_count, -1, per_group, BLOCK)
        return jnp.transpose(blocks, (0, 2, 1, 3)).reshape(leaf_count, per_group, row_count)
    return pl.pallas_call(
        reorder_kernel,
        out_shape=pltpu.VMEM(rows.shape, rows.dtype),
        in_specs=[pl.BlockSpec(memory_space=pltpu.SMEM), INSIDE],
        out_specs=INSIDE,
        compiler_params=pltpu.CompilerParams(vmem_limit_bytes=2 << 20),
    )(block_order, pltpu.with_memory_space_constraint(rows, pltpu.VMEM))


def weights_kernel(
    inverse_ref,
    inverse_far_ref,
    inverse_near_ref,
    inverse_last_ref,
    upper_ref,
    upper_near_ref,
    one_ref,
    basis_ref,
    inner_ref,
    coupling_ref,
    inverse_out,
    table_out,
    narrow_out,
    one,
    two_rows,
    three_rows,
    arrivals,
):
    bf16 = jnp.bfloat16
    share = lax.axis_index("rhs")
    position = lax.axis_index("leaf")
    span = inverse_ref.shape[0]
    rank = one.shape[0]
    copies = [pltpu.make_async_copy(one_ref, one, arrivals.at[0])]
    start = pl.multiple_of(share * span, 16)
    copies.append(
        pltpu.make_async_copy(inverse_ref, inverse_out.at[pl.ds(start, span), :], arrivals.at[1])
    )
    at = 0
    for index, piece in enumerate((basis_ref, inner_ref, coupling_ref)):
        height = piece.shape[0]
        copies.append(
            pltpu.make_async_copy(
                piece, narrow_out.at[pl.ds(at, height), :], arrivals.at[2 + index]
            )
        )
        at += height
    for copy in copies:
        copy.start()

    for flip, piece in ((2, inverse_far_ref), (1, inverse_near_ref), (3, inverse_last_ref)):
        start = pl.multiple_of((share ^ flip) * span, 16)
        inverse_out[pl.ds(start, span), :] = piece[...]

    two_half, three_half = rank // 4, rank // 8
    for flip, piece in ((0, upper_ref), (1, upper_near_ref)):
        half = share & 1 ^ flip
        at = 0
        for other in range(4):
            if other < 2:
                start = (position & 1 ^ other) * 2 * two_half + half * two_half
                start = pl.multiple_of(start, 16)
                two_rows[pl.ds(start, two_half), :] = piece[pl.ds(at, two_half), :]
                at += two_half
            start = (position & 3 ^ other) * 2 * three_half + half * three_half
            start = pl.multiple_of(start, 16)
            three_rows[pl.ds(start, three_half), :] = piece[pl.ds(at, three_half), :]
            at += three_half

    copies[0].wait()
    half = rank // 2
    at = narrow_out.shape[0] - rank
    narrow_out[pl.ds(at, rank), :half] = one[:, :half]
    narrow_out[pl.ds(at, rank), half:] = one[:, 2 * half : 3 * half]
    one_skeleton = jnp.concatenate([one[:, half : 2 * half], one[:, 3 * half :]], axis=1)
    through_two = product(one_skeleton, two_rows[...]).astype(bf16)
    width = rank // 4
    two_skeleton = jnp.concatenate(
        [through_two[:, (2 * g + 1) * width : (2 * g + 2) * width] for g in range(4)], axis=1
    )
    through_three = product(two_skeleton, three_rows[...]).astype(bf16)
    own_quad = position // 4 % 2
    for leaf in range(NODE_LEAVES):
        group = leaf % 4
        two = through_two[:, 2 * group * width : (2 * group + 1) * width]
        two = jnp.where(own_quad == leaf // 4, two, jnp.zeros_like(two))
        three = through_three[:, leaf * width : (leaf + 1) * width]
        table_out[:, leaf * 2 * width : (leaf + 1) * 2 * width] = jnp.concatenate(
            [three, two], axis=1
        )
    for copy in copies[1:]:
        copy.wait()


def weights_stage(inverse, inverse_pieces, upper, upper_near, one, basis, inner, coupling):
    rank = one.shape[0]
    bf16 = jnp.bfloat16
    span, extent = inverse.shape
    height = basis.shape[0] + inner.shape[0] + coupling.shape[0] + rank
    shapes = [(4 * span, extent), (rank, 4 * rank), (height, rank)]
    outside = pl.BlockSpec(memory_space=pl.ANY)

    def near(array):
        return pltpu.with_memory_space_constraint(array, pltpu.VMEM)

    def far(array):
        return pltpu.with_memory_space_constraint(array, pltpu.HBM)

    return pl.pallas_call(
        weights_kernel,
        out_shape=[pltpu.VMEM(shape, bf16) for shape in shapes],
        in_specs=[outside] + [INSIDE] * 5 + [outside] * 4,
        out_specs=[INSIDE] * 3,
        scratch_shapes=[pltpu.VMEM((rank, 2 * rank), bf16)] * 3 + [pltpu.SemaphoreType.DMA((5,))],
        compiler_params=pltpu.CompilerParams(vmem_limit_bytes=6 << 20),
    )(
        far(inverse),
        *map(near, inverse_pieces),
        near(upper),
        near(upper_near),
        far(one),
        far(basis),
        far(inner),
        far(coupling),
    )


def leaf_kernel(
    placed_ref, inverse_ref, table_ref, narrow_ref, eliminated_ref, terms_ref, kept_ref, sent_ref
):
    bf16 = jnp.bfloat16
    row_count = placed_ref.shape[1]
    split_at = inverse_ref.shape[0]
    rank = narrow_ref.shape[1]
    placed = placed_ref[...]
    basis = narrow_ref[:row_count]
    inner = narrow_ref[pl.ds(row_count, rank)]
    coupling = narrow_ref[pl.ds(row_count + rank, split_at)]
    one_eliminated = narrow_ref[pl.ds(row_count + rank + split_at, rank)]
    projected = product(placed, basis).astype(bf16)
    middle = product(projected, inner).astype(bf16)
    correction = product(middle, basis, ((1,), (1,)))
    reflected = (placed.astype(jnp.float32) - correction).astype(bf16)
    eliminated = product(reflected[:, :split_at], inverse_ref[...]).astype(bf16)
    eliminated_ref[...] = eliminated
    coupled = product(eliminated, coupling)
    skeleton = (reflected[:, split_at:].astype(jnp.float32) - coupled).astype(bf16)
    terms = product(skeleton, table_ref[...]).astype(bf16)
    width = terms_ref.shape[2]
    for leaf in range(terms_ref.shape[0]):
        terms_ref[leaf] = terms[:, leaf * width : (leaf + 1) * width]
    one_terms = product(skeleton, one_eliminated)
    half = one_terms.shape[1] // 2
    odd = lax.axis_index("leaf") & 1 == 1
    kept_ref[...] = jnp.where(odd, one_terms[:, half:], one_terms[:, :half])
    sent_ref[...] = jnp.where(odd, one_terms[:, :half], one_terms[:, half:])


def leaf_stage(placed, inverse, table, narrow):
    columns = placed.shape[0]
    rank = narrow.shape[1]
    return pl.pallas_call(
        leaf_kernel,
        out_shape=(
            jax.ShapeDtypeStruct((columns, inverse.shape[1]), jnp.bfloat16),
            jax.ShapeDtypeStruct((NODE_LEAVES, columns, rank // 2), jnp.bfloat16),
            pltpu.VMEM((columns, rank // 2), jnp.float32),
            pltpu.VMEM((columns, rank // 2), jnp.float32),
        ),
        in_specs=[INSIDE] * 4,
        out_specs=(INSIDE,) * 4,
        compiler_params=pltpu.CompilerParams(vmem_limit_bytes=6 << 20),
    )(placed, inverse, table, narrow)


def tail_kernel(received_ref, three_ref, top_ref, two_ref):
    total = jnp.sum(received_ref[...].astype(jnp.float32), axis=0).T
    eighth = three_ref.shape[0]
    three_ref[...] = total[:eighth]
    top_ref[...] = total[eighth : 2 * eighth]
    two_ref[...] = total[2 * eighth :]


def tail_stage(received):
    _, columns, width = received.shape
    return pl.pallas_call(
        tail_kernel,
        out_shape=[
            jax.ShapeDtypeStruct((width * part // 4, columns), jnp.float32) for part in (1, 1, 2)
        ],
        in_specs=[INSIDE],
        out_specs=[INSIDE] * 3,
        compiler_params=pltpu.CompilerParams(vmem_limit_bytes=2 << 20),
    )(received)


def shards(
    right_sides,
    block_order,
    leaf_basis,
    leaf_inner,
    leaf_inverse,
    leaf_coupling,
    merge_one,
    merge_two,
    merge_three,
):
    leaf_count = lax.axis_size("leaf")
    columns, row_count = right_sides.shape

    outgoing = right_sides.reshape(leaf_count, columns // leaf_count, row_count)
    arrived = lax.all_to_all(outgoing, "leaf", split_axis=0, concat_axis=0, tiled=True)

    inverse = leaf_inverse[0]
    inverse_far = exchanged(inverse, "rhs", 2)
    half = lax.axis_index("rhs") & 1
    two_half, three_half = merge_two.shape[0] // 2, merge_three.shape[0] // 2
    two = lax.dynamic_slice_in_dim(merge_two, half * two_half, two_half)
    three = lax.dynamic_slice_in_dim(merge_three, half * three_half, three_half)
    upper_own = jnp.concatenate([two, three], axis=0)
    upper_pieces = [upper_own, exchanged(upper_own, "leaf", 1)]
    upper_pieces += [exchanged(three, "leaf", flip) for flip in (2, 3)]
    upper = jnp.concatenate(upper_pieces, axis=0)

    inverse, inverse_far, upper, _ = lax.optimization_barrier(
        (inverse, inverse_far, upper, arrived)
    )
    inverse_near = exchanged(inverse, "rhs", 1)
    inverse_last = exchanged(inverse_far, "rhs", 1)
    upper_near = exchanged(upper, "rhs", 1)
    inverse_whole, table, narrow = weights_stage(
        leaf_inverse[0],
        (inverse_far, inverse_near, inverse_last),
        upper,
        upper_near,
        merge_one,
        leaf_basis[0],
        leaf_inner[0],
        leaf_coupling[0],
    )

    returning = reorder(arrived, block_order)
    placed = lax.all_to_all(returning, "leaf", split_axis=0, concat_axis=0, tiled=True).reshape(
        columns, row_count
    )
    eliminated, terms, kept, sent = leaf_stage(placed, inverse_whole, table, narrow)

    groups = None
    if leaf_count > NODE_LEAVES:
        groups = [list(range(i, i + NODE_LEAVES)) for i in range(0, leaf_count, NODE_LEAVES)]
    received = lax.all_to_all(
        terms, "leaf", split_axis=0, concat_axis=0, tiled=True, axis_index_groups=groups
    )
    level_one = kept + exchanged(sent, "leaf", 1)
    level_three, top_skeleton, level_two = (part.T for part in tail_stage(received))
    return (eliminated, level_one, level_two, level_three, top_skeleton)


def solution(mesh):
    placed = (
        P("rhs", "leaf"),
        P(),
        P("leaf", None, None),
        P("leaf", None, None),
        P("leaf", "rhs", None),
        P("leaf", None, None),
        P("leaf", None),
        P("leaf", None),
        P("leaf", None),
    )
    return jax.shard_map(
        shards,
        mesh=mesh,
        in_specs=placed,
        out_specs=(P("rhs", "leaf"),) * 5,
        check_vma=False,
    )
```

```python
import jax
import jax.numpy as jnp
from jax import lax
from jax.experimental import pallas as pl
from jax.experimental.pallas import tpu as pltpu
from jax.sharding import PartitionSpec as P

BLOCK = 128
NODE_LEAVES = 8
INSIDE = pl.BlockSpec(memory_space=pltpu.VMEM)
SCALARS = pl.BlockSpec(memory_space=pltpu.SMEM)
OUTSIDE = pl.BlockSpec(memory_space=pl.ANY)


def near(array):
    return pltpu.with_memory_space_constraint(array, pltpu.VMEM)


def far(array):
    return pltpu.with_memory_space_constraint(array, pltpu.HBM)


def exchanged(piece, axis, flip):
    count = lax.axis_size(axis)
    return lax.ppermute(piece, axis, [(i, i ^ flip) for i in range(count) if i ^ flip < count])


def product(left, right, over=((1,), (0,))):
    return lax.dot_general(left, right, (over, ((), ())), preferred_element_type=jnp.float32)


def reorder_kernel(order_ref, rows_ref, out_ref, staged, leaving):
    per_leaf = rows_ref.shape[2] // BLOCK
    copies = []
    for leaf in range(out_ref.shape[0]):
        for t in range(per_leaf):
            source = order_ref[leaf * per_leaf + t]
            column = pl.multiple_of(lax.rem(source, per_leaf) * BLOCK, BLOCK)
            staged[leaf, :, pl.ds(t * BLOCK, BLOCK)] = rows_ref[
                lax.div(source, per_leaf), :, pl.ds(column, BLOCK)
            ]
        copies.append(pltpu.make_async_copy(staged.at[leaf], out_ref.at[leaf], leaving.at[leaf]))
        copies[-1].start()
    for copy in copies:
        copy.wait()


def reorder(rows, block_order):
    leaf_count, per_group, row_count = rows.shape
    if per_group % 16 or leaf_count > 16:
        blocks = jnp.transpose(rows.reshape(leaf_count, per_group, -1, BLOCK), (0, 2, 1, 3))
        blocks = jnp.take(blocks.reshape(-1, per_group, BLOCK), block_order, axis=0)
        blocks = blocks.reshape(leaf_count, -1, per_group, BLOCK)
        return jnp.transpose(blocks, (0, 2, 1, 3)).reshape(leaf_count, per_group, row_count)
    return pl.pallas_call(
        reorder_kernel,
        out_shape=pltpu.HBM(rows.shape, rows.dtype),
        in_specs=[SCALARS, INSIDE],
        out_specs=OUTSIDE,
        scratch_shapes=[
            pltpu.VMEM(rows.shape, rows.dtype),
            pltpu.SemaphoreType.DMA((leaf_count,)),
        ],
        compiler_params=pltpu.CompilerParams(vmem_limit_bytes=2 << 20),
    )(pltpu.with_memory_space_constraint(block_order, pltpu.SMEM), near(rows))


def order_kernel(order_ref, order_out):
    def keep(t, carry):
        order_out[t] = order_ref[t]
        return carry

    lax.fori_loop(0, order_ref.shape[0], keep, 0, unroll=8)


def kept_order(block_order):
    return pl.pallas_call(
        order_kernel,
        out_shape=pltpu.SMEM(block_order.shape, block_order.dtype),
        in_specs=[SCALARS],
        out_specs=SCALARS,
        compiler_params=pltpu.CompilerParams(vmem_limit_bytes=1 << 20),
    )(block_order)


def halves_kernel(two_ref, three_ref, upper_out, three_out, arrivals):
    half = lax.axis_index("rhs") & 1
    two_half, three_half = two_ref.shape[0] // 2, three_ref.shape[0] // 2
    two = two_ref.at[pl.ds(pl.multiple_of(half * two_half, 16), two_half), :]
    three = three_ref.at[pl.ds(pl.multiple_of(half * three_half, 16), three_half), :]
    copies = [
        pltpu.make_async_copy(two, upper_out.at[pl.ds(0, two_half), :], arrivals.at[0]),
        pltpu.make_async_copy(three, upper_out.at[pl.ds(two_half, three_half), :], arrivals.at[1]),
        pltpu.make_async_copy(three, three_out, arrivals.at[2]),
    ]
    for copy in copies:
        copy.start()

    for copy in copies:
        copy.wait()


def halves(two, three):
    two_half, three_half, width = two.shape[0] // 2, three.shape[0] // 2, two.shape[1]
    return pl.pallas_call(
        halves_kernel,
        out_shape=[
            pltpu.VMEM((two_half + three_half, width), two.dtype),
            pltpu.VMEM((three_half, width), two.dtype),
        ],
        in_specs=[OUTSIDE] * 2,
        out_specs=[INSIDE] * 2,
        scratch_shapes=[pltpu.SemaphoreType.DMA((3,))],
        compiler_params=pltpu.CompilerParams(vmem_limit_bytes=1 << 20),
    )(far(two), far(three))


def weights_kernel(
    inverse_ref,
    inverse_far_ref,
    inverse_near_ref,
    inverse_last_ref,
    upper_ref,
    upper_near_ref,
    one_ref,
    basis_ref,
    inner_ref,
    coupling_ref,
    inverse_out,
    three_out,
    two_out,
    narrow_out,
    one,
    two_rows,
    three_rows,
    arrivals,
):
    bf16 = jnp.bfloat16
    share = lax.axis_index("rhs")
    position = lax.axis_index("leaf")
    span = inverse_ref.shape[0]
    rank = one.shape[0]
    copies = [pltpu.make_async_copy(one_ref, one, arrivals.at[0])]
    start = pl.multiple_of(share * span, 16)
    copies.append(
        pltpu.make_async_copy(inverse_ref, inverse_out.at[pl.ds(start, span), :], arrivals.at[1])
    )
    at = 0
    for index, piece in enumerate((basis_ref, inner_ref, coupling_ref)):
        height = piece.shape[0]
        copies.append(
            pltpu.make_async_copy(
                piece, narrow_out.at[pl.ds(at, height), :], arrivals.at[2 + index]
            )
        )
        at += height
    for copy in copies:
        copy.start()

    for flip, piece in ((2, inverse_far_ref), (1, inverse_near_ref), (3, inverse_last_ref)):
        start = pl.multiple_of((share ^ flip) * span, 16)
        inverse_out[pl.ds(start, span), :] = piece[...]

    two_half, three_half = rank // 4, rank // 8
    for flip, piece in ((0, upper_ref), (1, upper_near_ref)):
        half = share & 1 ^ flip
        at = 0
        for other in range(4):
            if other < 2:
                start = (position & 1 ^ other) * 2 * two_half + half * two_half
                start = pl.multiple_of(start, 16)
                two_rows[pl.ds(start, two_half), :] = piece[pl.ds(at, two_half), :]
                at += two_half
            start = (position & 3 ^ other) * 2 * three_half + half * three_half
            start = pl.multiple_of(start, 16)
            three_rows[pl.ds(start, three_half), :] = piece[pl.ds(at, three_half), :]
            at += three_half

    copies[0].wait()
    half = rank // 2
    at = narrow_out.shape[0] - rank
    narrow_out[pl.ds(at, rank), :half] = one[:, :half]
    narrow_out[pl.ds(at, rank), half:] = one[:, 2 * half : 3 * half]
    one_skeleton = jnp.concatenate([one[:, half : 2 * half], one[:, 3 * half :]], axis=1)
    through_two = product(one_skeleton, two_rows[...])
    width = rank // 4
    two_skeleton = jnp.concatenate(
        [through_two[:, (2 * g + 1) * width : (2 * g + 2) * width] for g in range(4)], axis=1
    ).astype(bf16)
    through_two = through_two.T.astype(bf16)
    for group in range(4):
        two_out[pl.ds(group * width, width), :] = through_two[
            2 * group * width : (2 * group + 1) * width
        ]
    three_out[...] = product(two_skeleton, three_rows[...]).T.astype(bf16)
    for copy in copies[1:]:
        copy.wait()


def weights_stage(inverse, inverse_pieces, upper, upper_near, one, basis, inner, coupling):
    rank = one.shape[0]
    bf16 = jnp.bfloat16
    span, extent = inverse.shape
    height = basis.shape[0] + inner.shape[0] + coupling.shape[0] + rank
    shapes = [(4 * span, extent), (2 * rank, rank), (rank, rank), (height, rank)]
    return pl.pallas_call(
        weights_kernel,
        out_shape=[pltpu.VMEM(shape, bf16) for shape in shapes],
        in_specs=[OUTSIDE] + [INSIDE] * 5 + [OUTSIDE] * 4,
        out_specs=[INSIDE] * 4,
        scratch_shapes=[pltpu.VMEM((rank, 2 * rank), bf16)] * 3 + [pltpu.SemaphoreType.DMA((5,))],
        cost_estimate=pl.CostEstimate(
            flops=10**9, bytes_accessed=6 * 10**6, transcendentals=0
        ),
        compiler_params=pltpu.CompilerParams(vmem_limit_bytes=6 << 20),
    )(
        far(inverse),
        *map(near, inverse_pieces),
        near(upper),
        near(upper_near),
        far(one),
        far(basis),
        far(inner),
        far(coupling),
    )


def leaf_kernel(
    placed_ref,
    inverse_ref,
    three_ref,
    two_ref,
    narrow_ref,
    eliminated_ref,
    terms_ref,
    near_ref,
    far_ref,
    last_ref,
    kept_one_ref,
    kept_two_ref,
    eliminated_staged,
    terms_staged,
    two_staged,
    leaving,
):
    bf16 = jnp.bfloat16
    row_count = placed_ref.shape[1]
    split_at = inverse_ref.shape[0]
    rank = narrow_ref.shape[1]
    placed = placed_ref[...]
    basis = narrow_ref[:row_count]
    inner = narrow_ref[pl.ds(row_count, rank)]
    coupling = narrow_ref[pl.ds(row_count + rank, split_at)]
    one_eliminated = narrow_ref[pl.ds(row_count + rank + split_at, rank)]
    projected = product(placed, basis).astype(bf16)
    middle = product(projected, inner).astype(bf16)
    correction = product(middle, basis, ((1,), (1,)))
    reflected = (placed.astype(jnp.float32) - correction).astype(bf16)
    eliminated = product(reflected[:, :split_at], inverse_ref[...]).astype(bf16)
    eliminated_staged[...] = eliminated
    copies = [pltpu.make_async_copy(eliminated_staged, eliminated_ref, leaving.at[0])]
    copies[0].start()
    coupled = product(eliminated, coupling)
    skeleton = (reflected[:, split_at:].astype(jnp.float32) - coupled).astype(bf16)
    terms = product(three_ref[...], skeleton, ((1,), (1,))).astype(bf16)
    terms_staged[...] = terms.reshape(terms_staged.shape)
    copies.append(pltpu.make_async_copy(terms_staged, terms_ref, leaving.at[1]))
    copies[1].start()

    position = lax.axis_index("leaf")
    one_terms = product(skeleton, one_eliminated)
    half = rank // 2
    odd = position & 1 == 1
    kept_one_ref[...] = jnp.where(odd, one_terms[:, half:], one_terms[:, :half])
    sent_one = jnp.where(odd, one_terms[:, :half], one_terms[:, half:]).astype(bf16)
    near_ref[pl.ds(0, sent_one.shape[0]), :] = sent_one
    two_staged[...] = product(two_ref[...], skeleton, ((1,), (1,))).reshape(two_staged.shape)
    own = position & 3
    kept_two_ref[...] = two_staged[own]
    near_ref[pl.ds(sent_one.shape[0], rank // 4), :] = two_staged[own ^ 1].astype(bf16)
    far_ref[...] = two_staged[own ^ 2].astype(bf16)
    last_ref[...] = two_staged[own ^ 3].astype(bf16)
    for copy in copies:
        copy.wait()


def leaf_stage(placed, inverse, three, two, narrow):
    columns = placed.shape[0]
    rank = narrow.shape[1]
    half, width = rank // 2, rank // 4
    f32, bf16 = jnp.float32, jnp.bfloat16
    return pl.pallas_call(
        leaf_kernel,
        out_shape=(
            pltpu.HBM((columns, inverse.shape[1]), bf16),
            pltpu.HBM((NODE_LEAVES, width, columns), bf16),
            pltpu.VMEM((columns + width, columns), bf16),
            pltpu.VMEM((width, columns), bf16),
            pltpu.VMEM((width, columns), bf16),
            pltpu.VMEM((columns, half), f32),
            pltpu.VMEM((width, columns), f32),
        ),
        in_specs=[INSIDE] * 5,
        out_specs=(OUTSIDE,) * 2 + (INSIDE,) * 5,
        scratch_shapes=[
            pltpu.VMEM((columns, inverse.shape[1]), bf16),
            pltpu.VMEM((NODE_LEAVES, width, columns), bf16),
            pltpu.VMEM((4, width, columns), f32),
            pltpu.SemaphoreType.DMA((2,)),
        ],
        compiler_params=pltpu.CompilerParams(vmem_limit_bytes=6 << 20),
    )(near(placed), near(inverse), near(three), near(two), near(narrow))


def tail_kernel(
    received_ref,
    near_ref,
    far_ref,
    last_ref,
    kept_one_ref,
    kept_two_ref,
    one_ref,
    two_ref,
    three_ref,
    top_ref,
):
    f32 = jnp.float32
    columns = kept_one_ref.shape[0]
    one_ref[...] = kept_one_ref[...] + near_ref[pl.ds(0, columns), :].astype(f32)
    two = kept_two_ref[...] + near_ref[pl.ds(columns, two_ref.shape[0]), :].astype(f32)
    two_ref[...] = two + far_ref[...].astype(f32) + last_ref[...].astype(f32)
    total = jnp.sum(received_ref[...].astype(f32), axis=0)
    three_ref[...] = total[: three_ref.shape[0]]
    top_ref[...] = total[three_ref.shape[0] :]


def tail_stage(received, *others):
    _, height, columns = received.shape
    kept_one, kept_two = others[-2:]
    shapes = [kept_one.shape, kept_two.shape] + [(height // 2, columns)] * 2
    return pl.pallas_call(
        tail_kernel,
        out_shape=[jax.ShapeDtypeStruct(shape, jnp.float32) for shape in shapes],
        in_specs=[INSIDE] * 6,
        out_specs=[INSIDE] * 4,
        compiler_params=pltpu.CompilerParams(vmem_limit_bytes=2 << 20),
    )(received, *others)


def shards(
    right_sides,
    block_order,
    leaf_basis,
    leaf_inner,
    leaf_inverse,
    leaf_coupling,
    merge_one,
    merge_two,
    merge_three,
):
    leaf_count = lax.axis_size("leaf")
    columns, row_count = right_sides.shape

    outgoing = right_sides.reshape(leaf_count, columns // leaf_count, row_count)
    arrived = lax.all_to_all(outgoing, "leaf", split_axis=0, concat_axis=0, tiled=True)

    upper_own, three = halves(merge_two, merge_three)
    upper_pieces = [upper_own, exchanged(upper_own, "leaf", 1)]
    upper_pieces += [exchanged(three, "leaf", flip) for flip in (2, 3)]
    inverse, block_order, _ = lax.optimization_barrier((leaf_inverse[0], block_order, upper_own))
    inverse_far = exchanged(inverse, "rhs", 2)
    order = kept_order(block_order)
    upper = jnp.concatenate(upper_pieces, axis=0)

    inverse, inverse_far, upper, _ = lax.optimization_barrier(
        (inverse, inverse_far, upper, arrived)
    )
    inverse_near = exchanged(inverse, "rhs", 1)
    inverse_last = exchanged(inverse_far, "rhs", 1)
    upper_near = exchanged(upper, "rhs", 1)
    inverse_whole, three_table, two_table, narrow = weights_stage(
        leaf_inverse[0],
        (inverse_far, inverse_near, inverse_last),
        upper,
        upper_near,
        merge_one,
        leaf_basis[0],
        leaf_inner[0],
        leaf_coupling[0],
    )

    returning = reorder(arrived, order)
    placed = lax.all_to_all(returning, "leaf", split_axis=0, concat_axis=0, tiled=True).reshape(
        columns, row_count
    )
    eliminated, terms, near_sent, far_sent, last_sent, kept_one, kept_two = leaf_stage(
        placed, inverse_whole, three_table, two_table, narrow
    )

    groups = None
    if leaf_count > NODE_LEAVES:
        groups = [list(range(i, i + NODE_LEAVES)) for i in range(0, leaf_count, NODE_LEAVES)]
    received = lax.all_to_all(
        terms, "leaf", split_axis=0, concat_axis=0, tiled=True, axis_index_groups=groups
    )
    level_one, level_two, level_three, top_skeleton = tail_stage(
        received,
        exchanged(near_sent, "leaf", 1),
        exchanged(far_sent, "leaf", 2),
        exchanged(last_sent, "leaf", 3),
        kept_one,
        kept_two,
    )
    return (eliminated, level_one, level_two.T, level_three.T, top_skeleton.T)


def solution(mesh):
    placed = (
        P("rhs", "leaf"),
        P(),
        P("leaf", None, None),
        P("leaf", None, None),
        P("leaf", "rhs", None),
        P("leaf", None, None),
        P("leaf", None),
        P("leaf", None),
        P("leaf", None),
    )
    return jax.shard_map(
        shards,
        mesh=mesh,
        in_specs=placed,
        out_specs=(P("rhs", "leaf"),) * 5,
        check_vma=False,
    )
```

```python
import jax
import jax.numpy as jnp
from jax import lax
from jax.experimental import pallas as pl
from jax.experimental.pallas import tpu as pltpu
from jax.sharding import PartitionSpec as P

BLOCK = 128
NODE_LEAVES = 8
MEMBERS = (4, 5, 1, 0, 7, 3, 6, 2)
LAST_MEMBERS = (4, 5, 1, 0, 7, 3, 6, 2)
INSIDE = pl.BlockSpec(memory_space=pltpu.VMEM)
SCALARS = pl.BlockSpec(memory_space=pltpu.SMEM)
OUTSIDE = pl.BlockSpec(memory_space=pl.ANY)


def near(array):
    return pltpu.with_memory_space_constraint(array, pltpu.VMEM)


def far(array):
    return pltpu.with_memory_space_constraint(array, pltpu.HBM)


def exchanged(piece, axis, flip):
    count = lax.axis_size(axis)
    return lax.ppermute(piece, axis, [(i, i ^ flip) for i in range(count) if i ^ flip < count])


def product(left, right, over=((1,), (0,))):
    return lax.dot_general(left, right, (over, ((), ())), preferred_element_type=jnp.float32)


def reorder_kernel(order_ref, rows_ref, out_ref, staged, leaving):
    per_leaf = rows_ref.shape[2] // BLOCK
    copies = []
    for slot, leaf in enumerate(MEMBERS):
        for t in range(per_leaf):
            source = order_ref[leaf * per_leaf + t]
            column = pl.multiple_of(lax.rem(source, per_leaf) * BLOCK, BLOCK)
            staged[slot, :, pl.ds(t * BLOCK, BLOCK)] = rows_ref[
                lax.div(source, per_leaf), :, pl.ds(column, BLOCK)
            ]
        copies.append(pltpu.make_async_copy(staged.at[slot], out_ref.at[slot], leaving.at[slot]))
        copies[-1].start()
    for copy in copies:
        copy.wait()


def reorder_anywhere(rows, block_order):
    leaf_count, per_group, row_count = rows.shape
    blocks = jnp.transpose(rows.reshape(leaf_count, per_group, -1, BLOCK), (0, 2, 1, 3))
    blocks = jnp.take(blocks.reshape(-1, per_group, BLOCK), block_order, axis=0)
    blocks = blocks.reshape(leaf_count, -1, per_group, BLOCK)
    return jnp.transpose(blocks, (0, 2, 1, 3)).reshape(leaf_count, per_group, row_count)


def reorder(rows, places):
    leaf_count = rows.shape[0]
    return pl.pallas_call(
        reorder_kernel,
        out_shape=pltpu.HBM(rows.shape, rows.dtype),
        in_specs=[SCALARS, INSIDE],
        out_specs=OUTSIDE,
        scratch_shapes=[
            pltpu.VMEM(rows.shape, rows.dtype),
            pltpu.SemaphoreType.DMA((leaf_count,)),
        ],
        compiler_params=pltpu.CompilerParams(vmem_limit_bytes=2 << 20),
    )(pltpu.with_memory_space_constraint(places, pltpu.SMEM), near(rows))


def early_kernel(order_ref, two_ref, three_ref, places_out, upper_out, three_out, arrivals):
    half = lax.axis_index("rhs") & 1
    two_half, three_half = two_ref.shape[0] // 2, three_ref.shape[0] // 2
    two = two_ref.at[pl.ds(pl.multiple_of(half * two_half, 16), two_half), :]
    three = three_ref.at[pl.ds(pl.multiple_of(half * three_half, 16), three_half), :]
    copies = [
        pltpu.make_async_copy(order_ref, places_out, arrivals.at[0]),
        pltpu.make_async_copy(two, upper_out.at[pl.ds(0, two_half), :], arrivals.at[1]),
        pltpu.make_async_copy(three, upper_out.at[pl.ds(two_half, three_half), :], arrivals.at[2]),
        pltpu.make_async_copy(three, three_out, arrivals.at[3]),
    ]
    for copy in copies:
        copy.start()
    copies[0].wait()
    leaves = len(MEMBERS)
    per_leaf = places_out.shape[0] // leaves
    slots = sum(slot << 3 * leaf for slot, leaf in enumerate(MEMBERS))

    def place(t, carry):
        source = places_out[t]
        leaf = lax.div(source, per_leaf)
        slot = lax.shift_right_logical(jnp.int32(slots), 3 * leaf) & 7
        places_out[t] = slot * per_leaf + lax.rem(source, per_leaf)
        return carry

    if per_leaf * leaves < 128:
        lax.fori_loop(0, per_leaf * leaves, place, 0, unroll=8)
    for copy in copies[1:]:
        copy.wait()


def early_stage(block_order, two, three):
    two_half, three_half, width = two.shape[0] // 2, three.shape[0] // 2, two.shape[1]
    return pl.pallas_call(
        early_kernel,
        out_shape=[
            pltpu.SMEM(block_order.shape, block_order.dtype),
            pltpu.VMEM((two_half + three_half, width), two.dtype),
            pltpu.VMEM((three_half, width), two.dtype),
        ],
        in_specs=[OUTSIDE] * 3,
        out_specs=[SCALARS] + [INSIDE] * 2,
        scratch_shapes=[pltpu.SemaphoreType.DMA((4,))],
        compiler_params=pltpu.CompilerParams(vmem_limit_bytes=1 << 20),
    )(far(block_order), far(two), far(three))


def weights_kernel(
    inverse_ref,
    inverse_far_ref,
    inverse_near_ref,
    inverse_last_ref,
    upper_ref,
    upper_near_ref,
    one_ref,
    basis_ref,
    inner_ref,
    coupling_ref,
    inverse_out,
    table_out,
    narrow_out,
    one,
    two_rows,
    three_rows,
    arrivals,
):
    bf16 = jnp.bfloat16
    share = lax.axis_index("rhs")
    position = lax.axis_index("leaf")
    span = inverse_ref.shape[0]
    rank = one.shape[0]
    copies = [pltpu.make_async_copy(one_ref, one, arrivals.at[0])]
    start = pl.multiple_of(share * span, 16)
    copies.append(
        pltpu.make_async_copy(inverse_ref, inverse_out.at[pl.ds(start, span), :], arrivals.at[1])
    )
    at = 0
    for index, piece in enumerate((basis_ref, inner_ref, coupling_ref)):
        height = piece.shape[0]
        copies.append(
            pltpu.make_async_copy(
                piece, narrow_out.at[pl.ds(at, height), :], arrivals.at[2 + index]
            )
        )
        at += height
    for copy in copies:
        copy.start()

    for flip, piece in ((2, inverse_far_ref), (1, inverse_near_ref), (3, inverse_last_ref)):
        start = pl.multiple_of((share ^ flip) * span, 16)
        inverse_out[pl.ds(start, span), :] = piece[...]

    two_half, three_half = rank // 4, rank // 8
    for flip, piece in ((0, upper_ref), (1, upper_near_ref)):
        half = share & 1 ^ flip
        at = 0
        for other in range(4):
            if other < 2:
                start = (position & 1 ^ other) * 2 * two_half + half * two_half
                start = pl.multiple_of(start, 16)
                two_rows[pl.ds(start, two_half), :] = piece[pl.ds(at, two_half), :]
                at += two_half
            start = (position & 3 ^ other) * 2 * three_half + half * three_half
            start = pl.multiple_of(start, 16)
            three_rows[pl.ds(start, three_half), :] = piece[pl.ds(at, three_half), :]
            at += three_half

    copies[0].wait()
    half = rank // 2
    at = narrow_out.shape[0] - rank
    narrow_out[pl.ds(at, rank), :half] = one[:, :half]
    narrow_out[pl.ds(at, rank), half:] = one[:, 2 * half : 3 * half]
    one_skeleton = jnp.concatenate([one[:, half : 2 * half], one[:, 3 * half :]], axis=1)
    through_two = product(one_skeleton, two_rows[...])
    width = rank // 4
    two_skeleton = jnp.concatenate(
        [through_two[:, (2 * g + 1) * width : (2 * g + 2) * width] for g in range(4)], axis=1
    ).astype(bf16)
    through_two = through_two.T.astype(bf16)
    through_three = product(two_skeleton, three_rows[...]).T.astype(bf16)
    own_quad = position // 4 % 2
    for slot, leaf in enumerate(LAST_MEMBERS):
        at = 2 * slot * width
        table_out[pl.ds(at, width), :] = through_three[leaf * width : (leaf + 1) * width]
        group = leaf % 4
        two = through_two[2 * group * width : (2 * group + 1) * width]
        two = jnp.where(own_quad == leaf // 4, two, jnp.zeros_like(two))
        table_out[pl.ds(at + width, width), :] = two
    for copy in copies[1:]:
        copy.wait()


def weights_stage(inverse, inverse_pieces, upper, upper_near, one, basis, inner, coupling):
    rank = one.shape[0]
    bf16 = jnp.bfloat16
    span, extent = inverse.shape
    height = basis.shape[0] + inner.shape[0] + coupling.shape[0] + rank
    shapes = [(4 * span, extent), (4 * rank, rank), (height, rank)]
    return pl.pallas_call(
        weights_kernel,
        out_shape=[pltpu.VMEM(shape, bf16) for shape in shapes],
        in_specs=[OUTSIDE] + [INSIDE] * 5 + [OUTSIDE] * 4,
        out_specs=[INSIDE] * 3,
        scratch_shapes=[pltpu.VMEM((rank, 2 * rank), bf16)] * 3 + [pltpu.SemaphoreType.DMA((5,))],
        cost_estimate=pl.CostEstimate(
            flops=10**9, bytes_accessed=6 * 10**6, transcendentals=0
        ),
        compiler_params=pltpu.CompilerParams(vmem_limit_bytes=6 << 20),
    )(
        far(inverse),
        *map(near, inverse_pieces),
        near(upper),
        near(upper_near),
        far(one),
        far(basis),
        far(inner),
        far(coupling),
    )


def leaf_kernel(
    placed_ref,
    inverse_ref,
    table_ref,
    narrow_ref,
    eliminated_ref,
    terms_ref,
    sent_one_ref,
    kept_one_ref,
    eliminated_staged,
    terms_staged,
    leaving,
):
    bf16 = jnp.bfloat16
    row_count = placed_ref.shape[1]
    split_at = inverse_ref.shape[0]
    rank = narrow_ref.shape[1]
    placed = placed_ref[...]
    basis = narrow_ref[:row_count]
    inner = narrow_ref[pl.ds(row_count, rank)]
    coupling = narrow_ref[pl.ds(row_count + rank, split_at)]
    one_eliminated = narrow_ref[pl.ds(row_count + rank + split_at, rank)]
    projected = product(placed, basis).astype(bf16)
    middle = product(projected, inner).astype(bf16)
    correction = product(middle, basis, ((1,), (1,)))
    reflected = (placed.astype(jnp.float32) - correction).astype(bf16)
    eliminated = product(reflected[:, :split_at], inverse_ref[...]).astype(bf16)
    eliminated_staged[...] = eliminated
    copies = [pltpu.make_async_copy(eliminated_staged, eliminated_ref, leaving.at[0])]
    copies[0].start()
    coupled = product(eliminated, coupling)
    skeleton = (reflected[:, split_at:].astype(jnp.float32) - coupled).astype(bf16)
    terms = product(table_ref[...], skeleton, ((1,), (1,))).astype(bf16)
    terms_staged[...] = terms.reshape(terms_staged.shape)
    copies.append(pltpu.make_async_copy(terms_staged, terms_ref, leaving.at[1]))
    copies[1].start()

    one_terms = product(skeleton, one_eliminated)
    half = rank // 2
    odd = lax.axis_index("leaf") & 1 == 1
    kept_one_ref[...] = jnp.where(odd, one_terms[:, half:], one_terms[:, :half])
    sent_one_ref[...] = jnp.where(odd, one_terms[:, :half], one_terms[:, half:]).astype(bf16)
    for copy in copies:
        copy.wait()


def leaf_stage(placed, inverse, table, narrow):
    columns = placed.shape[0]
    rank = narrow.shape[1]
    half = rank // 2
    bf16 = jnp.bfloat16
    return pl.pallas_call(
        leaf_kernel,
        out_shape=(
            pltpu.HBM((columns, inverse.shape[1]), bf16),
            pltpu.HBM((NODE_LEAVES, half, columns), bf16),
            pltpu.VMEM((columns, half), bf16),
            pltpu.VMEM((columns, half), jnp.float32),
        ),
        in_specs=[INSIDE] * 4,
        out_specs=(OUTSIDE,) * 2 + (INSIDE,) * 2,
        scratch_shapes=[
            pltpu.VMEM((columns, inverse.shape[1]), bf16),
            pltpu.VMEM((NODE_LEAVES, half, columns), bf16),
            pltpu.SemaphoreType.DMA((2,)),
        ],
        compiler_params=pltpu.CompilerParams(vmem_limit_bytes=6 << 20),
    )(near(placed), near(inverse), near(table), near(narrow))


def tail_kernel(
    received_ref, received_one_ref, kept_one_ref, one_ref, two_ref, three_ref, top_ref
):
    f32 = jnp.float32
    one_ref[...] = kept_one_ref[...] + received_one_ref[...].astype(f32)
    total = jnp.sum(received_ref[...].astype(f32), axis=0)
    eighth = three_ref.shape[0]
    three_ref[...] = total[:eighth]
    top_ref[...] = total[eighth : 2 * eighth]
    two_ref[...] = total[2 * eighth :]


def tail_stage(received, received_one, kept_one):
    _, height, columns = received.shape
    shapes = [kept_one.shape] + [(height // part, columns) for part in (2, 4, 4)]
    return pl.pallas_call(
        tail_kernel,
        out_shape=[jax.ShapeDtypeStruct(shape, jnp.float32) for shape in shapes],
        in_specs=[INSIDE] * 3,
        out_specs=[INSIDE] * 4,
        compiler_params=pltpu.CompilerParams(vmem_limit_bytes=2 << 20),
    )(received, received_one, kept_one)


def shards(
    right_sides,
    block_order,
    leaf_basis,
    leaf_inner,
    leaf_inverse,
    leaf_coupling,
    merge_one,
    merge_two,
    merge_three,
):
    leaf_count = lax.axis_size("leaf")
    columns, row_count = right_sides.shape

    one_node = leaf_count == NODE_LEAVES
    members = [list(MEMBERS)] if one_node else None

    def spread(pieces, groups):
        return lax.all_to_all(
            pieces, "leaf", split_axis=0, concat_axis=0, tiled=True, axis_index_groups=groups
        )

    arrived = spread(right_sides.reshape(leaf_count, columns // leaf_count, row_count), members)

    places, upper_own, three = early_stage(block_order, merge_two, merge_three)
    upper_pieces = [upper_own, exchanged(upper_own, "leaf", 1)]
    upper_pieces += [exchanged(three, "leaf", flip) for flip in (2, 3)]
    inverse, _ = lax.optimization_barrier((leaf_inverse[0], upper_own))
    inverse_far = exchanged(inverse, "rhs", 2)
    upper = jnp.concatenate(upper_pieces, axis=0)

    inverse, inverse_far, upper, _ = lax.optimization_barrier(
        (inverse, inverse_far, upper, arrived)
    )
    inverse_near = exchanged(inverse, "rhs", 1)
    inverse_last = exchanged(inverse_far, "rhs", 1)
    upper_near = exchanged(upper, "rhs", 1)
    inverse_whole, table, narrow = weights_stage(
        leaf_inverse[0],
        (inverse_far, inverse_near, inverse_last),
        upper,
        upper_near,
        merge_one,
        leaf_basis[0],
        leaf_inner[0],
        leaf_coupling[0],
    )

    if one_node:
        returning = reorder(arrived, places)
    else:
        returning = reorder_anywhere(arrived, block_order)
    placed = spread(returning, members).reshape(columns, row_count)
    eliminated, terms, sent_one, kept_one = leaf_stage(placed, inverse_whole, table, narrow)

    starts = range(0, leaf_count, NODE_LEAVES)
    received = spread(terms, [[start + leaf for leaf in LAST_MEMBERS] for start in starts])
    level_one, level_two, level_three, top_skeleton = tail_stage(
        received, exchanged(sent_one, "leaf", 1), kept_one
    )
    return (eliminated, level_one, level_two.T, level_three.T, top_skeleton.T)


def solution(mesh):
    placed = (
        P("rhs", "leaf"),
        P(),
        P("leaf", None, None),
        P("leaf", None, None),
        P("leaf", "rhs", None),
        P("leaf", None, None),
        P("leaf", None),
        P("leaf", None),
        P("leaf", None),
    )
    return jax.shard_map(
        shards,
        mesh=mesh,
        in_specs=placed,
        out_specs=(P("rhs", "leaf"),) * 5,
        check_vma=False,
    )
```

```python
import jax
import jax.numpy as jnp
from jax import lax
from jax.experimental import pallas as pl
from jax.experimental.pallas import tpu as pltpu
from jax.sharding import PartitionSpec as P

BLOCK = 128
NODE_LEAVES = 8
FIRST_MEMBERS = (4, 5, 6, 7, 0, 1, 2, 3)
MEMBERS = (4, 7, 3, 1, 0, 2, 6, 5)
LAST_MEMBERS = (5, 4, 1, 0, 7, 6, 3, 2)
INSIDE = pl.BlockSpec(memory_space=pltpu.VMEM)
SCALARS = pl.BlockSpec(memory_space=pltpu.SMEM)
OUTSIDE = pl.BlockSpec(memory_space=pl.ANY)


def near(array):
    return pltpu.with_memory_space_constraint(array, pltpu.VMEM)


def far(array):
    return pltpu.with_memory_space_constraint(array, pltpu.HBM)


def exchanged(piece, axis, flip):
    count = lax.axis_size(axis)
    return lax.ppermute(piece, axis, [(i, i ^ flip) for i in range(count) if i ^ flip < count])


def product(left, right, over=((1,), (0,))):
    return lax.dot_general(left, right, (over, ((), ())), preferred_element_type=jnp.float32)


def reorder_kernel(order_ref, rows_ref, out_ref, staged, leaving):
    per_leaf = rows_ref.shape[2] // BLOCK
    copies = []
    for slot, leaf in enumerate(MEMBERS):
        for t in range(per_leaf):
            source = order_ref[leaf * per_leaf + t]
            column = pl.multiple_of(lax.rem(source, per_leaf) * BLOCK, BLOCK)
            staged[slot, :, pl.ds(t * BLOCK, BLOCK)] = rows_ref[
                lax.div(source, per_leaf), :, pl.ds(column, BLOCK)
            ]
        copies.append(pltpu.make_async_copy(staged.at[slot], out_ref.at[slot], leaving.at[slot]))
        copies[-1].start()
    for copy in copies:
        copy.wait()


def reorder_anywhere(rows, block_order):
    leaf_count, per_group, row_count = rows.shape
    blocks = jnp.transpose(rows.reshape(leaf_count, per_group, -1, BLOCK), (0, 2, 1, 3))
    blocks = jnp.take(blocks.reshape(-1, per_group, BLOCK), block_order, axis=0)
    blocks = blocks.reshape(leaf_count, -1, per_group, BLOCK)
    return jnp.transpose(blocks, (0, 2, 1, 3)).reshape(leaf_count, per_group, row_count)


def reorder(rows, places):
    leaf_count = rows.shape[0]
    return pl.pallas_call(
        reorder_kernel,
        out_shape=pltpu.HBM(rows.shape, rows.dtype),
        in_specs=[SCALARS, INSIDE],
        out_specs=OUTSIDE,
        scratch_shapes=[
            pltpu.VMEM(rows.shape, rows.dtype),
            pltpu.SemaphoreType.DMA((leaf_count,)),
        ],
        compiler_params=pltpu.CompilerParams(vmem_limit_bytes=2 << 20),
    )(pltpu.with_memory_space_constraint(places, pltpu.SMEM), near(rows))


def early_kernel(order_ref, two_ref, three_ref, places_out, upper_out, three_out, arrivals):
    half = lax.axis_index("rhs") & 1
    two_half, three_half = two_ref.shape[0] // 2, three_ref.shape[0] // 2
    two = two_ref.at[pl.ds(pl.multiple_of(half * two_half, 16), two_half), :]
    three = three_ref.at[pl.ds(pl.multiple_of(half * three_half, 16), three_half), :]
    copies = [
        pltpu.make_async_copy(order_ref, places_out, arrivals.at[0]),
        pltpu.make_async_copy(two, upper_out.at[pl.ds(0, two_half), :], arrivals.at[1]),
        pltpu.make_async_copy(three, upper_out.at[pl.ds(two_half, three_half), :], arrivals.at[2]),
        pltpu.make_async_copy(three, three_out, arrivals.at[3]),
    ]
    for copy in copies:
        copy.start()
    copies[0].wait()
    leaves = len(FIRST_MEMBERS)
    per_leaf = places_out.shape[0] // leaves
    slots = sum(slot << 3 * leaf for slot, leaf in enumerate(FIRST_MEMBERS))

    def place(t, carry):
        source = places_out[t]
        leaf = lax.div(source, per_leaf)
        slot = lax.shift_right_logical(jnp.int32(slots), 3 * leaf) & 7
        places_out[t] = slot * per_leaf + lax.rem(source, per_leaf)
        return carry

    if per_leaf * leaves < 128:
        lax.fori_loop(0, per_leaf * leaves, place, 0, unroll=8)
    for copy in copies[1:]:
        copy.wait()


def early_stage(block_order, two, three):
    two_half, three_half, width = two.shape[0] // 2, three.shape[0] // 2, two.shape[1]
    return pl.pallas_call(
        early_kernel,
        out_shape=[
            pltpu.SMEM(block_order.shape, block_order.dtype),
            pltpu.VMEM((two_half + three_half, width), two.dtype),
            pltpu.VMEM((three_half, width), two.dtype),
        ],
        in_specs=[OUTSIDE] * 3,
        out_specs=[SCALARS] + [INSIDE] * 2,
        scratch_shapes=[pltpu.SemaphoreType.DMA((4,))],
        compiler_params=pltpu.CompilerParams(vmem_limit_bytes=1 << 20),
    )(far(block_order), far(two), far(three))


def weights_kernel(
    inverse_ref,
    inverse_far_ref,
    inverse_near_ref,
    inverse_last_ref,
    upper_ref,
    upper_near_ref,
    one_ref,
    basis_ref,
    inner_ref,
    coupling_ref,
    inverse_out,
    table_out,
    narrow_out,
    one,
    coupling,
    two_rows,
    three_rows,
    arrivals,
):
    bf16 = jnp.bfloat16
    share = lax.axis_index("rhs")
    position = lax.axis_index("leaf")
    span = inverse_ref.shape[0]
    rank = one.shape[0]
    copies = [pltpu.make_async_copy(one_ref, one, arrivals.at[0])]
    start = pl.multiple_of(share * span, 16)
    copies.append(
        pltpu.make_async_copy(inverse_ref, inverse_out.at[pl.ds(start, span), :], arrivals.at[1])
    )
    at = 0
    for index, piece in enumerate((basis_ref, inner_ref)):
        height = piece.shape[0]
        copies.append(
            pltpu.make_async_copy(
                piece, narrow_out.at[pl.ds(at, height), :], arrivals.at[2 + index]
            )
        )
        at += height
    copies.append(pltpu.make_async_copy(coupling_ref, coupling, arrivals.at[4]))
    for copy in copies:
        copy.start()

    for flip, piece in ((2, inverse_far_ref), (1, inverse_near_ref), (3, inverse_last_ref)):
        start = pl.multiple_of((share ^ flip) * span, 16)
        inverse_out[pl.ds(start, span), :] = piece[...]

    two_half, three_half = rank // 4, rank // 8
    for flip, piece in ((0, upper_ref), (1, upper_near_ref)):
        half = share & 1 ^ flip
        at = 0
        for other in range(4):
            if other < 2:
                start = (position & 1 ^ other) * 2 * two_half + half * two_half
                start = pl.multiple_of(start, 16)
                two_rows[pl.ds(start, two_half), :] = piece[pl.ds(at, two_half), :]
                at += two_half
            start = (position & 3 ^ other) * 2 * three_half + half * three_half
            start = pl.multiple_of(start, 16)
            three_rows[pl.ds(start, three_half), :] = piece[pl.ds(at, three_half), :]
            at += three_half

    copies[0].wait()
    half = rank // 2
    at = narrow_out.shape[0] - rank
    narrow_out[pl.ds(at, rank), :half] = one[:, :half]
    narrow_out[pl.ds(at, rank), half:] = one[:, 2 * half : 3 * half]
    one_skeleton = jnp.concatenate([one[:, half : 2 * half], one[:, 3 * half :]], axis=1)
    through_two = product(one_skeleton, two_rows[...])
    width = rank // 4
    two_skeleton = jnp.concatenate(
        [through_two[:, (2 * g + 1) * width : (2 * g + 2) * width] for g in range(4)], axis=1
    ).astype(bf16)
    through_two = through_two.T.astype(bf16)
    through_three = product(two_skeleton, three_rows[...]).T.astype(bf16)
    own_quad = position // 4 % 2
    for slot, leaf in enumerate(LAST_MEMBERS):
        at = 2 * slot * width
        table_out[pl.ds(at, width), :] = through_three[leaf * width : (leaf + 1) * width]
        group = leaf % 4
        two = through_two[2 * group * width : (2 * group + 1) * width]
        two = jnp.where(own_quad == leaf // 4, two, jnp.zeros_like(two))
        table_out[pl.ds(at + width, width), :] = two
    for copy in copies[1:]:
        copy.wait()
    height = coupling.shape[0]
    at = narrow_out.shape[0] - rank - height
    narrow_out[pl.ds(at, height), :] = product(inverse_out[...], coupling[...]).astype(bf16)


def weights_stage(inverse, inverse_pieces, upper, upper_near, one, basis, inner, coupling):
    rank = one.shape[0]
    bf16 = jnp.bfloat16
    span, extent = inverse.shape
    height = basis.shape[0] + inner.shape[0] + coupling.shape[0] + rank
    shapes = [(4 * span, extent), (4 * rank, rank), (height, rank)]
    return pl.pallas_call(
        weights_kernel,
        out_shape=[pltpu.VMEM(shape, bf16) for shape in shapes],
        in_specs=[OUTSIDE] + [INSIDE] * 5 + [OUTSIDE] * 4,
        out_specs=[INSIDE] * 3,
        scratch_shapes=[
            pltpu.VMEM((rank, 2 * rank), bf16),
            pltpu.VMEM(coupling.shape, bf16),
            pltpu.VMEM((rank, 2 * rank), bf16),
            pltpu.VMEM((rank, 2 * rank), bf16),
            pltpu.SemaphoreType.DMA((5,)),
        ],
        cost_estimate=pl.CostEstimate(
            flops=10**9, bytes_accessed=6 * 10**6, transcendentals=0
        ),
        compiler_params=pltpu.CompilerParams(vmem_limit_bytes=6 << 20),
    )(
        far(inverse),
        *map(near, inverse_pieces),
        near(upper),
        near(upper_near),
        far(one),
        far(basis),
        far(inner),
        far(coupling),
    )


def leaf_kernel(
    placed_ref,
    table_ref,
    narrow_ref,
    leading_ref,
    terms_ref,
    sent_one_ref,
    kept_one_ref,
    terms_staged,
    leaving,
):
    bf16 = jnp.bfloat16
    row_count = placed_ref.shape[2]
    rank = narrow_ref.shape[1]
    split_at = row_count - rank
    slots = range(placed_ref.shape[0])
    if len(slots) == NODE_LEAVES:
        slots = [MEMBERS.index(leaf) for leaf in FIRST_MEMBERS]
    placed = jnp.concatenate([placed_ref[slot] for slot in slots], axis=0)
    basis = narrow_ref[:row_count]
    inner = narrow_ref[pl.ds(row_count, rank)]
    through = narrow_ref[pl.ds(row_count + rank, split_at)]
    one_eliminated = narrow_ref[pl.ds(row_count + rank + split_at, rank)]
    projected = product(placed, basis).astype(bf16)
    middle = product(projected, inner).astype(bf16)
    correction = product(middle, basis, ((1,), (1,)))
    reflected = (placed.astype(jnp.float32) - correction).astype(bf16)
    leading = reflected[:, :split_at]
    leading_ref[...] = leading
    coupled = product(leading, through)
    skeleton = (reflected[:, split_at:].astype(jnp.float32) - coupled).astype(bf16)
    copies = []
    share = NODE_LEAVES // leaving.shape[0]
    height = terms_staged.shape[1]
    for part in range(leaving.shape[0]):
        table = table_ref[pl.ds(part * share * height, share * height), :]
        terms = product(table, skeleton, ((1,), (1,))).astype(bf16)
        some = pl.ds(part * share, share)
        terms_staged[some] = terms.reshape((share,) + terms_staged.shape[1:])
        copies.append(
            pltpu.make_async_copy(terms_staged.at[some], terms_ref.at[some], leaving.at[part])
        )
        copies[-1].start()

    one_terms = product(skeleton, one_eliminated)
    half = rank // 2
    odd = lax.axis_index("leaf") & 1 == 1
    kept_one_ref[...] = jnp.where(odd, one_terms[:, half:], one_terms[:, :half])
    sent_one_ref[...] = jnp.where(odd, one_terms[:, :half], one_terms[:, half:]).astype(bf16)
    for copy in copies:
        copy.wait()


def leaf_stage(placed, table, narrow):
    columns = placed.shape[0] * placed.shape[1]
    rank = narrow.shape[1]
    half = rank // 2
    bf16 = jnp.bfloat16
    return pl.pallas_call(
        leaf_kernel,
        out_shape=(
            pltpu.VMEM((columns, placed.shape[2] - rank), bf16),
            pltpu.HBM((NODE_LEAVES, half, columns), bf16),
            pltpu.VMEM((columns, half), bf16),
            pltpu.VMEM((columns, half), jnp.float32),
        ),
        in_specs=[INSIDE] * 3,
        out_specs=(INSIDE, OUTSIDE, INSIDE, INSIDE),
        scratch_shapes=[
            pltpu.VMEM((NODE_LEAVES, half, columns), bf16),
            pltpu.SemaphoreType.DMA((2,)),
        ],
        compiler_params=pltpu.CompilerParams(vmem_limit_bytes=6 << 20),
    )(near(placed), near(table), near(narrow))


def eliminate_kernel(leading_ref, inverse_ref, eliminated_ref):
    eliminated_ref[...] = product(leading_ref[...], inverse_ref[...]).astype(jnp.bfloat16)


def eliminate_stage(leading, inverse):
    return pl.pallas_call(
        eliminate_kernel,
        out_shape=jax.ShapeDtypeStruct(leading.shape, jnp.bfloat16),
        in_specs=[INSIDE] * 2,
        out_specs=INSIDE,
        cost_estimate=pl.CostEstimate(
            flops=10**9, bytes_accessed=6 * 10**6, transcendentals=0
        ),
        compiler_params=pltpu.CompilerParams(vmem_limit_bytes=6 << 20),
    )(near(leading), near(inverse))


def tail_kernel(
    received_ref, received_one_ref, kept_one_ref, one_ref, two_ref, three_ref, top_ref
):
    f32 = jnp.float32
    one_ref[...] = kept_one_ref[...] + received_one_ref[...].astype(f32)
    total = jnp.sum(received_ref[...].astype(f32), axis=0)
    eighth = three_ref.shape[0]
    three_ref[...] = total[:eighth]
    top_ref[...] = total[eighth : 2 * eighth]
    two_ref[...] = total[2 * eighth :]


def tail_stage(received, received_one, kept_one):
    _, height, columns = received.shape
    shapes = [kept_one.shape] + [(height // part, columns) for part in (2, 4, 4)]
    return pl.pallas_call(
        tail_kernel,
        out_shape=[jax.ShapeDtypeStruct(shape, jnp.float32) for shape in shapes],
        in_specs=[INSIDE] * 3,
        out_specs=[INSIDE] * 4,
        compiler_params=pltpu.CompilerParams(vmem_limit_bytes=2 << 20),
    )(received, received_one, kept_one)


def shards(
    right_sides,
    block_order,
    leaf_basis,
    leaf_inner,
    leaf_inverse,
    leaf_coupling,
    merge_one,
    merge_two,
    merge_three,
):
    leaf_count = lax.axis_size("leaf")
    columns, row_count = right_sides.shape

    one_node = leaf_count == NODE_LEAVES
    first_members, members = ([list(FIRST_MEMBERS)], [list(MEMBERS)]) if one_node else (None, None)

    def spread(pieces, groups):
        return lax.all_to_all(
            pieces, "leaf", split_axis=0, concat_axis=0, tiled=True, axis_index_groups=groups
        )

    arrived = spread(right_sides.reshape(leaf_count, columns // leaf_count, row_count), first_members)

    places, upper_own, three = early_stage(block_order, merge_two, merge_three)
    upper_pieces = [upper_own, exchanged(upper_own, "leaf", 1)]
    upper_pieces += [exchanged(three, "leaf", flip) for flip in (2, 3)]
    inverse, _ = lax.optimization_barrier((leaf_inverse[0], upper_own))
    inverse_far = exchanged(inverse, "rhs", 2)
    upper = jnp.concatenate(upper_pieces, axis=0)

    inverse, inverse_far, upper, _ = lax.optimization_barrier(
        (inverse, inverse_far, upper, arrived)
    )
    inverse_near = exchanged(inverse, "rhs", 1)
    inverse_last = exchanged(inverse_far, "rhs", 1)
    upper_near = exchanged(upper, "rhs", 1)
    inverse_whole, table, narrow = weights_stage(
        leaf_inverse[0],
        (inverse_far, inverse_near, inverse_last),
        upper,
        upper_near,
        merge_one,
        leaf_basis[0],
        leaf_inner[0],
        leaf_coupling[0],
    )

    if one_node:
        returning = reorder(arrived, places)
    else:
        returning = reorder_anywhere(arrived, block_order)
    placed = spread(returning, members)
    leading, terms, sent_one, kept_one = leaf_stage(placed, table, narrow)

    starts = range(0, leaf_count, NODE_LEAVES)
    received = spread(terms, [[start + leaf for leaf in LAST_MEMBERS] for start in starts])
    eliminated = eliminate_stage(leading, inverse_whole)
    level_one, level_two, level_three, top_skeleton = tail_stage(
        received, exchanged(sent_one, "leaf", 1), kept_one
    )
    return (eliminated, level_one, level_two.T, level_three.T, top_skeleton.T)


def solution(mesh):
    placed = (
        P("rhs", "leaf"),
        P(),
        P("leaf", None, None),
        P("leaf", None, None),
        P("leaf", "rhs", None),
        P("leaf", None, None),
        P("leaf", None),
        P("leaf", None),
        P("leaf", None),
    )
    return jax.shard_map(
        shards,
        mesh=mesh,
        in_specs=placed,
        out_specs=(P("rhs", "leaf"),) * 5,
        check_vma=False,
    )
```

```python
import jax
import jax.numpy as jnp
from jax import lax
from jax.experimental import pallas as pl
from jax.experimental.pallas import tpu as pltpu
from jax.sharding import PartitionSpec as P

BLOCK = 128
NODE_LEAVES = 8
FIRST_MEMBERS = (4, 5, 6, 7, 0, 1, 2, 3)
MEMBERS = (4, 7, 3, 1, 0, 2, 6, 5)
LAST_MEMBERS = (5, 4, 1, 0, 7, 6, 3, 2)
INSIDE = pl.BlockSpec(memory_space=pltpu.VMEM)
SCALARS = pl.BlockSpec(memory_space=pltpu.SMEM)
OUTSIDE = pl.BlockSpec(memory_space=pl.ANY)


def near(array):
    return pltpu.with_memory_space_constraint(array, pltpu.VMEM)


def far(array):
    return pltpu.with_memory_space_constraint(array, pltpu.HBM)


def exchanged(piece, axis, flip):
    count = lax.axis_size(axis)
    return lax.ppermute(piece, axis, [(i, i ^ flip) for i in range(count) if i ^ flip < count])


def product(left, right, over=((1,), (0,))):
    return lax.dot_general(left, right, (over, ((), ())), preferred_element_type=jnp.float32)


def reorder_kernel(order_ref, rows_ref, out_ref, staged, leaving):
    per_leaf = rows_ref.shape[2] // BLOCK
    copies = []
    arrived_slots = sum(slot << 3 * leaf for slot, leaf in enumerate(FIRST_MEMBERS))
    for slot, leaf in enumerate(MEMBERS):
        for t in range(per_leaf):
            source = order_ref[leaf * per_leaf + t]
            column = pl.multiple_of(lax.rem(source, per_leaf) * BLOCK, BLOCK)
            from_slot = lax.shift_right_logical(
                jnp.int32(arrived_slots), 3 * lax.div(source, per_leaf)
            )
            staged[slot, :, pl.ds(t * BLOCK, BLOCK)] = rows_ref[
                from_slot & 7, :, pl.ds(column, BLOCK)
            ]
        copies.append(pltpu.make_async_copy(staged.at[slot], out_ref.at[slot], leaving.at[slot]))
        copies[-1].start()
    for copy in copies:
        copy.wait()


def reorder_anywhere(rows, block_order):
    leaf_count, per_group, row_count = rows.shape
    blocks = jnp.transpose(rows.reshape(leaf_count, per_group, -1, BLOCK), (0, 2, 1, 3))
    blocks = jnp.take(blocks.reshape(-1, per_group, BLOCK), block_order, axis=0)
    blocks = blocks.reshape(leaf_count, -1, per_group, BLOCK)
    return jnp.transpose(blocks, (0, 2, 1, 3)).reshape(leaf_count, per_group, row_count)


def reorder(rows, order_kept):
    leaf_count = rows.shape[0]
    return pl.pallas_call(
        reorder_kernel,
        out_shape=pltpu.HBM(rows.shape, rows.dtype),
        in_specs=[SCALARS, INSIDE],
        out_specs=OUTSIDE,
        scratch_shapes=[
            pltpu.VMEM(rows.shape, rows.dtype),
            pltpu.SemaphoreType.DMA((leaf_count,)),
        ],
        compiler_params=pltpu.CompilerParams(vmem_limit_bytes=2 << 20),
    )(pltpu.with_memory_space_constraint(order_kept, pltpu.SMEM), near(rows))


def early_kernel(order_ref, two_ref, three_ref, order_kept_out, upper_out, three_out, arrivals):
    half = lax.axis_index("rhs") & 1
    two_half, three_half = two_ref.shape[0] // 2, three_ref.shape[0] // 2
    two = two_ref.at[pl.ds(pl.multiple_of(half * two_half, 16), two_half), :]
    three = three_ref.at[pl.ds(pl.multiple_of(half * three_half, 16), three_half), :]
    copies = [
        pltpu.make_async_copy(order_ref, order_kept_out, arrivals.at[0]),
        pltpu.make_async_copy(two, upper_out.at[pl.ds(0, two_half), :], arrivals.at[1]),
        pltpu.make_async_copy(three, upper_out.at[pl.ds(two_half, three_half), :], arrivals.at[2]),
        pltpu.make_async_copy(three, three_out, arrivals.at[3]),
    ]
    for copy in copies:
        copy.start()
    for copy in copies:
        copy.wait()


def early_stage(block_order, two, three):
    two_half, three_half, width = two.shape[0] // 2, three.shape[0] // 2, two.shape[1]
    return pl.pallas_call(
        early_kernel,
        out_shape=[
            pltpu.SMEM(block_order.shape, block_order.dtype),
            pltpu.VMEM((two_half + three_half, width), two.dtype),
            pltpu.VMEM((three_half, width), two.dtype),
        ],
        in_specs=[OUTSIDE] * 3,
        out_specs=[SCALARS] + [INSIDE] * 2,
        scratch_shapes=[pltpu.SemaphoreType.DMA((4,))],
        compiler_params=pltpu.CompilerParams(vmem_limit_bytes=1 << 20),
    )(far(block_order), far(two), far(three))


def weights_kernel(
    inverse_ref,
    inverse_far_ref,
    inverse_near_ref,
    inverse_last_ref,
    upper_ref,
    upper_near_ref,
    one_ref,
    basis_ref,
    inner_ref,
    coupling_ref,
    inverse_out,
    table_out,
    narrow_out,
    one,
    coupling,
    two_rows,
    three_rows,
    arrivals,
):
    bf16 = jnp.bfloat16
    share = lax.axis_index("rhs")
    position = lax.axis_index("leaf")
    span = inverse_ref.shape[0]
    rank = one.shape[0]
    start = pl.multiple_of(share * span, 16)
    copies = [
        pltpu.make_async_copy(one_ref, one, arrivals.at[0]),
        pltpu.make_async_copy(coupling_ref, coupling, arrivals.at[1]),
        pltpu.make_async_copy(inverse_ref, inverse_out.at[pl.ds(start, span), :], arrivals.at[2]),
    ]
    at = 0
    for index, piece in enumerate((basis_ref, inner_ref)):
        place = narrow_out.at[pl.ds(at, piece.shape[0]), :]
        copies.append(pltpu.make_async_copy(piece, place, arrivals.at[3 + index]))
        at += piece.shape[0]
    for copy in copies:
        copy.start()

    for flip, piece in ((2, inverse_far_ref), (1, inverse_near_ref), (3, inverse_last_ref)):
        start = pl.multiple_of((share ^ flip) * span, 16)
        inverse_out[pl.ds(start, span), :] = piece[...]

    two_half, three_half = rank // 4, rank // 8
    for flip, piece in ((0, upper_ref), (1, upper_near_ref)):
        half = share & 1 ^ flip
        at = 0
        for other in range(4):
            if other < 2:
                start = (position & 1 ^ other) * 2 * two_half + half * two_half
                start = pl.multiple_of(start, 16)
                two_rows[pl.ds(start, two_half), :] = piece[pl.ds(at, two_half), :]
                at += two_half
            start = (position & 3 ^ other) * 2 * three_half + half * three_half
            start = pl.multiple_of(start, 16)
            three_rows[pl.ds(start, three_half), :] = piece[pl.ds(at, three_half), :]
            at += three_half

    copies[0].wait()
    half = rank // 2
    at = narrow_out.shape[0] - rank
    narrow_out[pl.ds(at, rank), :half] = one[:, :half]
    narrow_out[pl.ds(at, rank), half:] = one[:, 2 * half : 3 * half]
    one_skeleton = jnp.concatenate([one[:, half : 2 * half], one[:, 3 * half :]], axis=1)
    through_two = product(one_skeleton, two_rows[...])
    width = rank // 4
    two_skeleton = jnp.concatenate(
        [through_two[:, (2 * g + 1) * width : (2 * g + 2) * width] for g in range(4)], axis=1
    )
    two_high = two_skeleton.astype(bf16)
    two_low = (two_skeleton - two_high.astype(jnp.float32)).astype(bf16)
    through_two = through_two.T.astype(bf16)
    three = three_rows[...]
    through_three = (product(two_high, three) + product(two_low, three)).T.astype(bf16)
    own_quad = position // 4 % 2
    for slot, leaf in enumerate(LAST_MEMBERS):
        at = 2 * slot * width
        table_out[pl.ds(at, width), :] = through_three[leaf * width : (leaf + 1) * width]
        group = leaf % 4
        two = through_two[2 * group * width : (2 * group + 1) * width]
        two = jnp.where(own_quad == leaf // 4, two, jnp.zeros_like(two))
        table_out[pl.ds(at + width, width), :] = two
    for copy in copies[1:3]:
        copy.wait()
    height = coupling.shape[0]
    at = narrow_out.shape[0] - rank - height
    narrow_out[pl.ds(at, height), :] = product(inverse_out[...], coupling[...]).astype(bf16)
    for copy in copies[3:]:
        copy.wait()


def weights_stage(inverse, inverse_pieces, upper, upper_near, one, basis, inner, coupling):
    rank = one.shape[0]
    bf16 = jnp.bfloat16
    span, extent = inverse.shape
    height = basis.shape[0] + inner.shape[0] + coupling.shape[0] + rank
    shapes = [(4 * span, extent), (4 * rank, rank), (height, rank)]
    return pl.pallas_call(
        weights_kernel,
        out_shape=[pltpu.VMEM(shape, bf16) for shape in shapes],
        in_specs=[OUTSIDE] + [INSIDE] * 5 + [OUTSIDE] * 4,
        out_specs=[INSIDE] * 3,
        scratch_shapes=[
            pltpu.VMEM((rank, 2 * rank), bf16),
            pltpu.VMEM(coupling.shape, bf16),
            pltpu.VMEM((rank, 2 * rank), bf16),
            pltpu.VMEM((rank, 2 * rank), bf16),
            pltpu.SemaphoreType.DMA((5,)),
        ],
        cost_estimate=pl.CostEstimate(
            flops=10**9, bytes_accessed=6 * 10**6, transcendentals=0
        ),
        compiler_params=pltpu.CompilerParams(vmem_limit_bytes=6 << 20),
    )(
        far(inverse),
        *map(near, inverse_pieces),
        near(upper),
        near(upper_near),
        far(one),
        far(basis),
        far(inner),
        far(coupling),
    )


def leaf_kernel(
    placed_ref,
    table_ref,
    narrow_ref,
    leading_ref,
    terms_ref,
    sent_one_ref,
    kept_one_ref,
    terms_staged,
    leaving,
):
    bf16 = jnp.bfloat16
    row_count = placed_ref.shape[2]
    rank = narrow_ref.shape[1]
    split_at = row_count - rank
    slots = range(placed_ref.shape[0])
    if len(slots) == NODE_LEAVES:
        slots = [MEMBERS.index(leaf) for leaf in FIRST_MEMBERS]
    placed = jnp.concatenate([placed_ref[slot] for slot in slots], axis=0)
    basis = narrow_ref[:row_count]
    inner = narrow_ref[pl.ds(row_count, rank)]
    through = narrow_ref[pl.ds(row_count + rank, split_at)]
    one_eliminated = narrow_ref[pl.ds(row_count + rank + split_at, rank)]
    projected = product(placed, basis).astype(bf16)
    middle = product(projected, inner).astype(bf16)
    correction = product(middle, basis, ((1,), (1,)))
    reflected = (placed.astype(jnp.float32) - correction).astype(bf16)
    leading = reflected[:, :split_at]
    leading_ref[...] = leading
    coupled = product(leading, through)
    skeleton = (reflected[:, split_at:].astype(jnp.float32) - coupled).astype(bf16)
    copies = []
    share = NODE_LEAVES // leaving.shape[0]
    height = terms_staged.shape[1]
    for part in range(leaving.shape[0]):
        table = table_ref[pl.ds(part * share * height, share * height), :]
        terms = product(table, skeleton, ((1,), (1,))).astype(bf16)
        some = pl.ds(part * share, share)
        terms_staged[some] = terms.reshape((share,) + terms_staged.shape[1:])
        copies.append(
            pltpu.make_async_copy(terms_staged.at[some], terms_ref.at[some], leaving.at[part])
        )
        copies[-1].start()

    one_terms = product(skeleton, one_eliminated)
    half = rank // 2
    odd = lax.axis_index("leaf") & 1 == 1
    kept_one_ref[...] = jnp.where(odd, one_terms[:, half:], one_terms[:, :half])
    sent_one_ref[...] = jnp.where(odd, one_terms[:, :half], one_terms[:, half:]).astype(bf16)
    for copy in copies:
        copy.wait()


def leaf_stage(placed, table, narrow):
    columns = placed.shape[0] * placed.shape[1]
    rank = narrow.shape[1]
    half = rank // 2
    bf16 = jnp.bfloat16
    return pl.pallas_call(
        leaf_kernel,
        out_shape=(
            pltpu.VMEM((columns, placed.shape[2] - rank), bf16),
            pltpu.HBM((NODE_LEAVES, half, columns), bf16),
            pltpu.VMEM((columns, half), bf16),
            pltpu.VMEM((columns, half), jnp.float32),
        ),
        in_specs=[INSIDE] * 3,
        out_specs=(INSIDE, OUTSIDE, INSIDE, INSIDE),
        scratch_shapes=[
            pltpu.VMEM((NODE_LEAVES, half, columns), bf16),
            pltpu.SemaphoreType.DMA((4,)),
        ],
        compiler_params=pltpu.CompilerParams(vmem_limit_bytes=6 << 20),
    )(near(placed), near(table), near(narrow))


def eliminate_kernel(leading_ref, inverse_ref, eliminated_ref):
    eliminated_ref[...] = product(leading_ref[...], inverse_ref[...]).astype(jnp.bfloat16)


def eliminate_stage(leading, inverse):
    return pl.pallas_call(
        eliminate_kernel,
        out_shape=jax.ShapeDtypeStruct(leading.shape, jnp.bfloat16),
        in_specs=[INSIDE] * 2,
        out_specs=INSIDE,
        cost_estimate=pl.CostEstimate(
            flops=10**9, bytes_accessed=6 * 10**6, transcendentals=0
        ),
        compiler_params=pltpu.CompilerParams(vmem_limit_bytes=6 << 20),
    )(near(leading), near(inverse))


def tail_kernel(
    received_ref, received_one_ref, kept_one_ref, one_ref, two_ref, three_ref, top_ref
):
    f32 = jnp.float32
    one_ref[...] = kept_one_ref[...] + received_one_ref[...].astype(f32)
    total = jnp.sum(received_ref[...].astype(f32), axis=0)
    eighth = three_ref.shape[0]
    three_ref[...] = total[:eighth]
    top_ref[...] = total[eighth : 2 * eighth]
    two_ref[...] = total[2 * eighth :]


def tail_stage(received, received_one, kept_one):
    _, height, columns = received.shape
    shapes = [kept_one.shape] + [(height // part, columns) for part in (2, 4, 4)]
    return pl.pallas_call(
        tail_kernel,
        out_shape=[jax.ShapeDtypeStruct(shape, jnp.float32) for shape in shapes],
        in_specs=[INSIDE] * 3,
        out_specs=[INSIDE] * 4,
        compiler_params=pltpu.CompilerParams(vmem_limit_bytes=2 << 20),
    )(received, received_one, kept_one)


def shards(
    right_sides,
    block_order,
    leaf_basis,
    leaf_inner,
    leaf_inverse,
    leaf_coupling,
    merge_one,
    merge_two,
    merge_three,
):
    leaf_count = lax.axis_size("leaf")
    columns, row_count = right_sides.shape

    one_node = leaf_count == NODE_LEAVES
    first_members, members = ([list(FIRST_MEMBERS)], [list(MEMBERS)]) if one_node else (None, None)

    def spread(pieces, groups):
        return lax.all_to_all(
            pieces, "leaf", split_axis=0, concat_axis=0, tiled=True, axis_index_groups=groups
        )

    arrived = spread(right_sides.reshape(leaf_count, columns // leaf_count, row_count), first_members)

    order_kept, upper_own, three = early_stage(block_order, merge_two, merge_three)
    upper_pieces = [upper_own, exchanged(upper_own, "leaf", 1)]
    upper_pieces += [exchanged(three, "leaf", flip) for flip in (2, 3)]
    inverse, _ = lax.optimization_barrier((leaf_inverse[0], upper_own))
    inverse_far = exchanged(inverse, "rhs", 2)
    upper = jnp.concatenate(upper_pieces, axis=0)

    inverse, inverse_far, upper, _ = lax.optimization_barrier(
        (inverse, inverse_far, upper, arrived)
    )
    inverse_near = exchanged(inverse, "rhs", 1)
    inverse_last = exchanged(inverse_far, "rhs", 1)
    upper_near = exchanged(upper, "rhs", 1)
    inverse_whole, table, narrow = weights_stage(
        leaf_inverse[0],
        (inverse_far, inverse_near, inverse_last),
        upper,
        upper_near,
        merge_one,
        leaf_basis[0],
        leaf_inner[0],
        leaf_coupling[0],
    )

    if one_node:
        returning = reorder(arrived, order_kept)
    else:
        returning = reorder_anywhere(arrived, block_order)
    placed = spread(returning, members)
    leading, terms, sent_one, kept_one = leaf_stage(placed, table, narrow)

    starts = range(0, leaf_count, NODE_LEAVES)
    received = spread(terms, [[start + leaf for leaf in LAST_MEMBERS] for start in starts])
    eliminated = eliminate_stage(leading, inverse_whole)
    level_one, level_two, level_three, top_skeleton = tail_stage(
        received, exchanged(sent_one, "leaf", 1), kept_one
    )
    return (eliminated, level_one, level_two.T, level_three.T, top_skeleton.T)


def solution(mesh):
    placed = (
        P("rhs", "leaf"),
        P(),
        P("leaf", None, None),
        P("leaf", None, None),
        P("leaf", "rhs", None),
        P("leaf", None, None),
        P("leaf", None),
        P("leaf", None),
        P("leaf", None),
    )
    return jax.shard_map(
        shards,
        mesh=mesh,
        in_specs=placed,
        out_specs=(P("rhs", "leaf"),) * 5,
        check_vma=False,
    )
```

```python
import jax
import jax.numpy as jnp
from jax import lax
from jax.experimental import pallas as pl
from jax.experimental.pallas import tpu as pltpu
from jax.sharding import PartitionSpec as P

BLOCK = 128
NODE_LEAVES = 8
FIRST_MEMBERS = (4, 5, 6, 7, 0, 1, 2, 3)
MEMBERS = (4, 2, 3, 5, 0, 6, 7, 1)
LAST_MEMBERS = (5, 4, 1, 0, 7, 6, 3, 2)
INSIDE = pl.BlockSpec(memory_space=pltpu.VMEM)
SCALARS = pl.BlockSpec(memory_space=pltpu.SMEM)
OUTSIDE = pl.BlockSpec(memory_space=pl.ANY)


def near(array):
    return pltpu.with_memory_space_constraint(array, pltpu.VMEM)


def far(array):
    return pltpu.with_memory_space_constraint(array, pltpu.HBM)


def exchanged(piece, axis, flip):
    count = lax.axis_size(axis)
    return lax.ppermute(piece, axis, [(i, i ^ flip) for i in range(count) if i ^ flip < count])


def product(left, right, over=((1,), (0,))):
    return lax.dot_general(left, right, (over, ((), ())), preferred_element_type=jnp.float32)


def reorder_kernel(order_ref, rows_ref, out_ref, staged, leaving):
    per_leaf = rows_ref.shape[2] // BLOCK
    copies = []
    arrived_slots = sum(slot << 3 * leaf for slot, leaf in enumerate(FIRST_MEMBERS))
    for slot, leaf in enumerate(MEMBERS):
        for t in range(per_leaf):
            source = order_ref[leaf * per_leaf + t]
            column = pl.multiple_of(lax.rem(source, per_leaf) * BLOCK, BLOCK)
            from_slot = lax.shift_right_logical(
                jnp.int32(arrived_slots), 3 * lax.div(source, per_leaf)
            )
            staged[slot, :, pl.ds(t * BLOCK, BLOCK)] = rows_ref[
                from_slot & 7, :, pl.ds(column, BLOCK)
            ]
        copies.append(pltpu.make_async_copy(staged.at[slot], out_ref.at[slot], leaving.at[slot]))
        copies[-1].start()
    for copy in copies:
        copy.wait()


def reorder_anywhere(rows, block_order):
    leaf_count, per_group, row_count = rows.shape
    blocks = jnp.transpose(rows.reshape(leaf_count, per_group, -1, BLOCK), (0, 2, 1, 3))
    blocks = jnp.take(blocks.reshape(-1, per_group, BLOCK), block_order, axis=0)
    blocks = blocks.reshape(leaf_count, -1, per_group, BLOCK)
    return jnp.transpose(blocks, (0, 2, 1, 3)).reshape(leaf_count, per_group, row_count)


def reorder(rows, order_kept):
    leaf_count = rows.shape[0]
    return pl.pallas_call(
        reorder_kernel,
        out_shape=pltpu.HBM(rows.shape, rows.dtype),
        in_specs=[SCALARS, INSIDE],
        out_specs=OUTSIDE,
        scratch_shapes=[
            pltpu.VMEM(rows.shape, rows.dtype),
            pltpu.SemaphoreType.DMA((leaf_count,)),
        ],
        compiler_params=pltpu.CompilerParams(vmem_limit_bytes=2 << 20),
    )(pltpu.with_memory_space_constraint(order_kept, pltpu.SMEM), near(rows))


def early_kernel(order_ref, two_ref, three_ref, order_kept_out, upper_out, three_out, arrivals):
    half = lax.axis_index("rhs") & 1
    two_half, three_half = two_ref.shape[0] // 2, three_ref.shape[0] // 2
    two = two_ref.at[pl.ds(pl.multiple_of(half * two_half, 16), two_half), :]
    three = three_ref.at[pl.ds(pl.multiple_of(half * three_half, 16), three_half), :]
    copies = [
        pltpu.make_async_copy(order_ref, order_kept_out, arrivals.at[0]),
        pltpu.make_async_copy(two, upper_out.at[pl.ds(0, two_half), :], arrivals.at[1]),
        pltpu.make_async_copy(three, upper_out.at[pl.ds(two_half, three_half), :], arrivals.at[2]),
        pltpu.make_async_copy(three, three_out, arrivals.at[3]),
    ]
    for copy in copies:
        copy.start()
    for copy in copies:
        copy.wait()


def early_stage(block_order, two, three):
    two_half, three_half, width = two.shape[0] // 2, three.shape[0] // 2, two.shape[1]
    return pl.pallas_call(
        early_kernel,
        out_shape=[
            pltpu.SMEM(block_order.shape, block_order.dtype),
            pltpu.VMEM((two_half + three_half, width), two.dtype),
            pltpu.VMEM((three_half, width), two.dtype),
        ],
        in_specs=[OUTSIDE] * 3,
        out_specs=[SCALARS] + [INSIDE] * 2,
        scratch_shapes=[pltpu.SemaphoreType.DMA((4,))],
        compiler_params=pltpu.CompilerParams(vmem_limit_bytes=1 << 20),
    )(far(block_order), far(two), far(three))


def weights_kernel(
    inverse_ref,
    inverse_far_ref,
    inverse_near_ref,
    inverse_last_ref,
    upper_ref,
    upper_near_ref,
    one_ref,
    basis_ref,
    inner_ref,
    coupling_ref,
    inverse_out,
    table_out,
    narrow_out,
    one,
    coupling,
    two_rows,
    three_rows,
    arrivals,
):
    bf16 = jnp.bfloat16
    share = lax.axis_index("rhs")
    position = lax.axis_index("leaf")
    span = inverse_ref.shape[0]
    rank = one.shape[0]
    start = pl.multiple_of(share * span, 16)
    copies = [
        pltpu.make_async_copy(one_ref, one, arrivals.at[0]),
        pltpu.make_async_copy(coupling_ref, coupling, arrivals.at[1]),
        pltpu.make_async_copy(inverse_ref, inverse_out.at[pl.ds(start, span), :], arrivals.at[2]),
    ]
    at = 0
    for index, piece in enumerate((basis_ref, inner_ref)):
        place = narrow_out.at[pl.ds(at, piece.shape[0]), :]
        copies.append(pltpu.make_async_copy(piece, place, arrivals.at[3 + index]))
        at += piece.shape[0]
    for copy in copies:
        copy.start()

    for flip, piece in ((2, inverse_far_ref), (1, inverse_near_ref), (3, inverse_last_ref)):
        start = pl.multiple_of((share ^ flip) * span, 16)
        inverse_out[pl.ds(start, span), :] = piece[...]

    two_half, three_half = rank // 4, rank // 8
    for flip, piece in ((0, upper_ref), (1, upper_near_ref)):
        half = share & 1 ^ flip
        at = 0
        for other in range(4):
            if other < 2:
                start = (position & 1 ^ other) * 2 * two_half + half * two_half
                start = pl.multiple_of(start, 16)
                two_rows[pl.ds(start, two_half), :] = piece[pl.ds(at, two_half), :]
                at += two_half
            start = (position & 3 ^ other) * 2 * three_half + half * three_half
            start = pl.multiple_of(start, 16)
            three_rows[pl.ds(start, three_half), :] = piece[pl.ds(at, three_half), :]
            at += three_half

    copies[0].wait()
    half = rank // 2
    at = narrow_out.shape[0] - rank
    narrow_out[pl.ds(at, rank), :half] = one[:, :half]
    narrow_out[pl.ds(at, rank), half:] = one[:, 2 * half : 3 * half]
    one_skeleton = jnp.concatenate([one[:, half : 2 * half], one[:, 3 * half :]], axis=1)
    through_two = product(one_skeleton, two_rows[...])
    width = rank // 4
    two_skeleton = jnp.concatenate(
        [through_two[:, (2 * g + 1) * width : (2 * g + 2) * width] for g in range(4)], axis=1
    )
    two_high = two_skeleton.astype(bf16)
    two_low = (two_skeleton - two_high.astype(jnp.float32)).astype(bf16)
    through_two = through_two.T.astype(bf16)
    three = three_rows[...]
    through_three = (product(two_high, three) + product(two_low, three)).T.astype(bf16)
    own_quad = position // 4 % 2
    for slot, leaf in enumerate(LAST_MEMBERS):
        at = 2 * slot * width
        table_out[pl.ds(at, width), :] = through_three[leaf * width : (leaf + 1) * width]
        group = leaf % 4
        two = through_two[2 * group * width : (2 * group + 1) * width]
        two = jnp.where(own_quad == leaf // 4, two, jnp.zeros_like(two))
        table_out[pl.ds(at + width, width), :] = two
    for copy in copies[1:3]:
        copy.wait()
    height = coupling.shape[0]
    at = narrow_out.shape[0] - rank - height
    narrow_out[pl.ds(at, height), :] = product(inverse_out[...], coupling[...]).astype(bf16)
    for copy in copies[3:]:
        copy.wait()


def weights_stage(inverse, inverse_pieces, upper, upper_near, one, basis, inner, coupling):
    rank = one.shape[0]
    bf16 = jnp.bfloat16
    span, extent = inverse.shape
    height = basis.shape[0] + inner.shape[0] + coupling.shape[0] + rank
    shapes = [(4 * span, extent), (4 * rank, rank), (height, rank)]
    return pl.pallas_call(
        weights_kernel,
        out_shape=[pltpu.VMEM(shape, bf16) for shape in shapes],
        in_specs=[OUTSIDE] + [INSIDE] * 5 + [OUTSIDE] * 4,
        out_specs=[INSIDE] * 3,
        scratch_shapes=[
            pltpu.VMEM((rank, 2 * rank), bf16),
            pltpu.VMEM(coupling.shape, bf16),
            pltpu.VMEM((rank, 2 * rank), bf16),
            pltpu.VMEM((rank, 2 * rank), bf16),
            pltpu.SemaphoreType.DMA((5,)),
        ],
        cost_estimate=pl.CostEstimate(
            flops=10**9, bytes_accessed=6 * 10**6, transcendentals=0
        ),
        compiler_params=pltpu.CompilerParams(vmem_limit_bytes=6 << 20),
    )(
        far(inverse),
        *map(near, inverse_pieces),
        near(upper),
        near(upper_near),
        far(one),
        far(basis),
        far(inner),
        far(coupling),
    )


def leaf_kernel(
    placed_ref,
    table_ref,
    narrow_ref,
    leading_ref,
    terms_ref,
    sent_one_ref,
    kept_one_ref,
    terms_staged,
    leaving,
):
    bf16 = jnp.bfloat16
    row_count = placed_ref.shape[2]
    rank = narrow_ref.shape[1]
    split_at = row_count - rank
    slots = range(placed_ref.shape[0])
    if len(slots) == NODE_LEAVES:
        slots = [MEMBERS.index(leaf) for leaf in FIRST_MEMBERS]
    placed = jnp.concatenate([placed_ref[slot] for slot in slots], axis=0)
    basis = narrow_ref[:row_count]
    inner = narrow_ref[pl.ds(row_count, rank)]
    through = narrow_ref[pl.ds(row_count + rank, split_at)]
    one_eliminated = narrow_ref[pl.ds(row_count + rank + split_at, rank)]
    projected = product(placed, basis).astype(bf16)
    middle = product(projected, inner).astype(bf16)
    correction = product(middle, basis, ((1,), (1,)))
    reflected = (placed.astype(jnp.float32) - correction).astype(bf16)
    leading = reflected[:, :split_at]
    leading_ref[...] = leading
    coupled = product(leading, through)
    skeleton = (reflected[:, split_at:].astype(jnp.float32) - coupled).astype(bf16)
    copies = []
    share = NODE_LEAVES // leaving.shape[0]
    height = terms_staged.shape[1]
    for part in range(leaving.shape[0]):
        table = table_ref[pl.ds(part * share * height, share * height), :]
        terms = product(table, skeleton, ((1,), (1,))).astype(bf16)
        some = pl.ds(part * share, share)
        terms_staged[some] = terms.reshape((share,) + terms_staged.shape[1:])
        copies.append(
            pltpu.make_async_copy(terms_staged.at[some], terms_ref.at[some], leaving.at[part])
        )
        copies[-1].start()

    one_terms = product(skeleton, one_eliminated)
    half = rank // 2
    odd = lax.axis_index("leaf") & 1 == 1
    kept_one_ref[...] = jnp.where(odd, one_terms[:, half:], one_terms[:, :half])
    sent_one_ref[...] = jnp.where(odd, one_terms[:, :half], one_terms[:, half:]).astype(bf16)
    for copy in copies:
        copy.wait()


def leaf_stage(placed, table, narrow):
    columns = placed.shape[0] * placed.shape[1]
    rank = narrow.shape[1]
    half = rank // 2
    bf16 = jnp.bfloat16
    return pl.pallas_call(
        leaf_kernel,
        out_shape=(
            pltpu.VMEM((columns, placed.shape[2] - rank), bf16),
            pltpu.HBM((NODE_LEAVES, half, columns), bf16),
            pltpu.VMEM((columns, half), bf16),
            pltpu.VMEM((columns, half), jnp.float32),
        ),
        in_specs=[INSIDE] * 3,
        out_specs=(INSIDE, OUTSIDE, INSIDE, INSIDE),
        scratch_shapes=[
            pltpu.VMEM((NODE_LEAVES, half, columns), bf16),
            pltpu.SemaphoreType.DMA((4,)),
        ],
        compiler_params=pltpu.CompilerParams(vmem_limit_bytes=6 << 20),
    )(near(placed), near(table), near(narrow))


def eliminate_kernel(leading_ref, inverse_ref, eliminated_ref):
    eliminated_ref[...] = product(leading_ref[...], inverse_ref[...]).astype(jnp.bfloat16)


def eliminate_stage(leading, inverse):
    return pl.pallas_call(
        eliminate_kernel,
        out_shape=jax.ShapeDtypeStruct(leading.shape, jnp.bfloat16),
        in_specs=[INSIDE] * 2,
        out_specs=INSIDE,
        cost_estimate=pl.CostEstimate(
            flops=10**9, bytes_accessed=6 * 10**6, transcendentals=0
        ),
        compiler_params=pltpu.CompilerParams(vmem_limit_bytes=6 << 20),
    )(near(leading), near(inverse))


def tail_kernel(
    received_ref, received_one_ref, kept_one_ref, one_ref, two_ref, three_ref, top_ref
):
    f32 = jnp.float32
    one_ref[...] = kept_one_ref[...] + received_one_ref[...].astype(f32)
    total = jnp.sum(received_ref[...].astype(f32), axis=0)
    eighth = three_ref.shape[0]
    three_ref[...] = total[:eighth]
    top_ref[...] = total[eighth : 2 * eighth]
    two_ref[...] = total[2 * eighth :]


def tail_stage(received, received_one, kept_one):
    _, height, columns = received.shape
    shapes = [kept_one.shape] + [(height // part, columns) for part in (2, 4, 4)]
    return pl.pallas_call(
        tail_kernel,
        out_shape=[jax.ShapeDtypeStruct(shape, jnp.float32) for shape in shapes],
        in_specs=[INSIDE] * 3,
        out_specs=[INSIDE] * 4,
        compiler_params=pltpu.CompilerParams(vmem_limit_bytes=2 << 20),
    )(received, received_one, kept_one)


def shards(
    right_sides,
    block_order,
    leaf_basis,
    leaf_inner,
    leaf_inverse,
    leaf_coupling,
    merge_one,
    merge_two,
    merge_three,
):
    leaf_count = lax.axis_size("leaf")
    columns, row_count = right_sides.shape

    one_node = leaf_count == NODE_LEAVES
    first_members, members = ([list(FIRST_MEMBERS)], [list(MEMBERS)]) if one_node else (None, None)

    def spread(pieces, groups):
        return lax.all_to_all(
            pieces, "leaf", split_axis=0, concat_axis=0, tiled=True, axis_index_groups=groups
        )

    arrived = spread(right_sides.reshape(leaf_count, columns // leaf_count, row_count), first_members)

    order_kept, upper_own, three = early_stage(block_order, merge_two, merge_three)
    upper_pieces = [upper_own, exchanged(upper_own, "leaf", 1)]
    upper_pieces += [exchanged(three, "leaf", flip) for flip in (2, 3)]
    inverse, _ = lax.optimization_barrier((leaf_inverse[0], upper_own))
    inverse_far = exchanged(inverse, "rhs", 2)
    upper = jnp.concatenate(upper_pieces, axis=0)

    inverse, inverse_far, upper, _ = lax.optimization_barrier(
        (inverse, inverse_far, upper, arrived)
    )
    inverse_near = exchanged(inverse, "rhs", 1)
    inverse_last = exchanged(inverse_far, "rhs", 1)
    upper_near = exchanged(upper, "rhs", 1)
    inverse_whole, table, narrow = weights_stage(
        leaf_inverse[0],
        (inverse_far, inverse_near, inverse_last),
        upper,
        upper_near,
        merge_one,
        leaf_basis[0],
        leaf_inner[0],
        leaf_coupling[0],
    )

    if one_node:
        returning = reorder(arrived, order_kept)
    else:
        returning = reorder_anywhere(arrived, block_order)
    placed = spread(returning, members)
    leading, terms, sent_one, kept_one = leaf_stage(placed, table, narrow)

    starts = range(0, leaf_count, NODE_LEAVES)
    received = spread(terms, [[start + leaf for leaf in LAST_MEMBERS] for start in starts])
    eliminated = eliminate_stage(leading, inverse_whole)
    level_one, level_two, level_three, top_skeleton = tail_stage(
        received, exchanged(sent_one, "leaf", 1), kept_one
    )
    return (eliminated, level_one, level_two.T, level_three.T, top_skeleton.T)


def solution(mesh):
    placed = (
        P("rhs", "leaf"),
        P(),
        P("leaf", None, None),
        P("leaf", None, None),
        P("leaf", "rhs", None),
        P("leaf", None, None),
        P("leaf", None),
        P("leaf", None),
        P("leaf", None),
    )
    return jax.shard_map(
        shards,
        mesh=mesh,
        in_specs=placed,
        out_specs=(P("rhs", "leaf"),) * 5,
        check_vma=False,
    )
```

```python
import jax
import jax.numpy as jnp
from jax import lax
from jax.experimental import pallas as pl
from jax.experimental.pallas import tpu as pltpu
from jax.sharding import PartitionSpec as P

BLOCK = 128
NODE_LEAVES = 8
FIRST_MEMBERS = (4, 5, 6, 7, 0, 1, 2, 3)
MEMBERS = (4, 2, 3, 5, 0, 6, 7, 1)
LAST_MEMBERS = (5, 4, 1, 0, 7, 6, 3, 2)
INSIDE = pl.BlockSpec(memory_space=pltpu.VMEM)
SCALARS = pl.BlockSpec(memory_space=pltpu.SMEM)
OUTSIDE = pl.BlockSpec(memory_space=pl.ANY)


def near(array):
    return pltpu.with_memory_space_constraint(array, pltpu.VMEM)


def far(array):
    return pltpu.with_memory_space_constraint(array, pltpu.HBM)


def exchanged(piece, axis, flip):
    count = lax.axis_size(axis)
    return lax.ppermute(piece, axis, [(i, i ^ flip) for i in range(count) if i ^ flip < count])


def product(left, right, over=((1,), (0,))):
    return lax.dot_general(left, right, (over, ((), ())), preferred_element_type=jnp.float32)


def reorder_kernel(order_ref, rows_ref, out_ref, staged, leaving):
    per_leaf = rows_ref.shape[2] // BLOCK
    copies = []
    bits = per_leaf.bit_length() - 1
    arrived_slots = sum(slot << 3 * leaf for slot, leaf in enumerate(FIRST_MEMBERS))
    for slot, leaf in enumerate(MEMBERS):
        for t in range(per_leaf):
            source = order_ref[leaf * per_leaf + t]
            column = pl.multiple_of((source & per_leaf - 1) * BLOCK, BLOCK)
            from_slot = lax.shift_right_logical(jnp.int32(arrived_slots), (source >> bits) * 3)
            staged[slot, :, pl.ds(t * BLOCK, BLOCK)] = rows_ref[
                from_slot & 7, :, pl.ds(column, BLOCK)
            ]
        copies.append(pltpu.make_async_copy(staged.at[slot], out_ref.at[slot], leaving.at[slot]))
        copies[-1].start()
    for copy in copies:
        copy.wait()


def reorder_anywhere(rows, block_order):
    leaf_count, per_group, row_count = rows.shape
    blocks = jnp.transpose(rows.reshape(leaf_count, per_group, -1, BLOCK), (0, 2, 1, 3))
    blocks = jnp.take(blocks.reshape(-1, per_group, BLOCK), block_order, axis=0)
    blocks = blocks.reshape(leaf_count, -1, per_group, BLOCK)
    return jnp.transpose(blocks, (0, 2, 1, 3)).reshape(leaf_count, per_group, row_count)


def reorder(rows, order_kept):
    leaf_count = rows.shape[0]
    return pl.pallas_call(
        reorder_kernel,
        out_shape=pltpu.HBM(rows.shape, rows.dtype),
        in_specs=[SCALARS, INSIDE],
        out_specs=OUTSIDE,
        scratch_shapes=[
            pltpu.VMEM(rows.shape, rows.dtype),
            pltpu.SemaphoreType.DMA((leaf_count,)),
        ],
        compiler_params=pltpu.CompilerParams(vmem_limit_bytes=2 << 20),
    )(pltpu.with_memory_space_constraint(order_kept, pltpu.SMEM), near(rows))


def early_kernel(order_ref, two_ref, three_ref, order_kept_out, upper_out, three_out, arrivals):
    half = lax.axis_index("rhs") & 1
    two_half, three_half = two_ref.shape[0] // 2, three_ref.shape[0] // 2
    two = two_ref.at[pl.ds(pl.multiple_of(half * two_half, 16), two_half), :]
    three = three_ref.at[pl.ds(pl.multiple_of(half * three_half, 16), three_half), :]
    copies = [
        pltpu.make_async_copy(order_ref, order_kept_out, arrivals.at[0]),
        pltpu.make_async_copy(two, upper_out.at[pl.ds(0, two_half), :], arrivals.at[1]),
        pltpu.make_async_copy(three, upper_out.at[pl.ds(two_half, three_half), :], arrivals.at[2]),
        pltpu.make_async_copy(three, three_out, arrivals.at[3]),
    ]
    for copy in copies:
        copy.start()
    for copy in copies:
        copy.wait()


def early_stage(block_order, two, three):
    two_half, three_half, width = two.shape[0] // 2, three.shape[0] // 2, two.shape[1]
    return pl.pallas_call(
        early_kernel,
        out_shape=[
            pltpu.SMEM(block_order.shape, block_order.dtype),
            pltpu.VMEM((two_half + three_half, width), two.dtype),
            pltpu.VMEM((three_half, width), two.dtype),
        ],
        in_specs=[OUTSIDE] * 3,
        out_specs=[SCALARS] + [INSIDE] * 2,
        scratch_shapes=[pltpu.SemaphoreType.DMA((4,))],
        compiler_params=pltpu.CompilerParams(vmem_limit_bytes=1 << 20),
    )(far(block_order), far(two), far(three))


def weights_kernel(
    inverse_ref,
    inverse_far_ref,
    inverse_near_ref,
    inverse_last_ref,
    upper_ref,
    upper_near_ref,
    one_ref,
    basis_ref,
    inner_ref,
    coupling_ref,
    inverse_out,
    table_out,
    narrow_out,
    one,
    coupling,
    two_rows,
    three_rows,
    arrivals,
):
    bf16 = jnp.bfloat16
    share = lax.axis_index("rhs")
    position = lax.axis_index("leaf")
    span = inverse_ref.shape[0]
    rank = one.shape[0]
    start = pl.multiple_of(share * span, 16)
    copies = [
        pltpu.make_async_copy(one_ref, one, arrivals.at[0]),
        pltpu.make_async_copy(coupling_ref, coupling, arrivals.at[1]),
        pltpu.make_async_copy(inverse_ref, inverse_out.at[pl.ds(start, span), :], arrivals.at[2]),
    ]
    at = 0
    for index, piece in enumerate((basis_ref, inner_ref)):
        place = narrow_out.at[pl.ds(at, piece.shape[0]), :]
        copies.append(pltpu.make_async_copy(piece, place, arrivals.at[3 + index]))
        at += piece.shape[0]
    for copy in copies:
        copy.start()

    for flip, piece in ((2, inverse_far_ref), (1, inverse_near_ref), (3, inverse_last_ref)):
        start = pl.multiple_of((share ^ flip) * span, 16)
        inverse_out[pl.ds(start, span), :] = piece[...]

    two_half, three_half = rank // 4, rank // 8
    for flip, piece in ((0, upper_ref), (1, upper_near_ref)):
        half = share & 1 ^ flip
        at = 0
        for other in range(4):
            if other < 2:
                start = (position & 1 ^ other) * 2 * two_half + half * two_half
                start = pl.multiple_of(start, 16)
                two_rows[pl.ds(start, two_half), :] = piece[pl.ds(at, two_half), :]
                at += two_half
            start = (position & 3 ^ other) * 2 * three_half + half * three_half
            start = pl.multiple_of(start, 16)
            three_rows[pl.ds(start, three_half), :] = piece[pl.ds(at, three_half), :]
            at += three_half

    copies[0].wait()
    half = rank // 2
    at = narrow_out.shape[0] - rank
    narrow_out[pl.ds(at, rank), :half] = one[:, :half]
    narrow_out[pl.ds(at, rank), half:] = one[:, 2 * half : 3 * half]
    one_skeleton = jnp.concatenate([one[:, half : 2 * half], one[:, 3 * half :]], axis=1)
    through_two = product(one_skeleton, two_rows[...])
    width = rank // 4
    two_skeleton = jnp.concatenate(
        [through_two[:, (2 * g + 1) * width : (2 * g + 2) * width] for g in range(4)], axis=1
    )
    two_high = two_skeleton.astype(bf16)
    two_low = (two_skeleton - two_high.astype(jnp.float32)).astype(bf16)
    through_two = through_two.T.astype(bf16)
    three = three_rows[...]
    through_three = (product(two_high, three) + product(two_low, three)).T.astype(bf16)
    own_quad = position // 4 % 2
    for slot, leaf in enumerate(LAST_MEMBERS):
        at = 2 * slot * width
        table_out[pl.ds(at, width), :] = through_three[leaf * width : (leaf + 1) * width]
        group = leaf % 4
        two = through_two[2 * group * width : (2 * group + 1) * width]
        two = jnp.where(own_quad == leaf // 4, two, jnp.zeros_like(two))
        table_out[pl.ds(at + width, width), :] = two
    for copy in copies[1:3]:
        copy.wait()
    height = coupling.shape[0]
    at = narrow_out.shape[0] - rank - height
    narrow_out[pl.ds(at, height), :] = product(inverse_out[...], coupling[...]).astype(bf16)
    for copy in copies[3:]:
        copy.wait()


def weights_stage(inverse, inverse_pieces, upper, upper_near, one, basis, inner, coupling):
    rank = one.shape[0]
    bf16 = jnp.bfloat16
    span, extent = inverse.shape
    height = basis.shape[0] + inner.shape[0] + coupling.shape[0] + rank
    shapes = [(4 * span, extent), (4 * rank, rank), (height, rank)]
    return pl.pallas_call(
        weights_kernel,
        out_shape=[pltpu.VMEM(shape, bf16) for shape in shapes],
        in_specs=[OUTSIDE] + [INSIDE] * 5 + [OUTSIDE] * 4,
        out_specs=[INSIDE] * 3,
        scratch_shapes=[
            pltpu.VMEM((rank, 2 * rank), bf16),
            pltpu.VMEM(coupling.shape, bf16),
            pltpu.VMEM((rank, 2 * rank), bf16),
            pltpu.VMEM((rank, 2 * rank), bf16),
            pltpu.SemaphoreType.DMA((5,)),
        ],
        cost_estimate=pl.CostEstimate(
            flops=10**9, bytes_accessed=6 * 10**6, transcendentals=0
        ),
        compiler_params=pltpu.CompilerParams(vmem_limit_bytes=6 << 20),
    )(
        far(inverse),
        *map(near, inverse_pieces),
        near(upper),
        near(upper_near),
        far(one),
        far(basis),
        far(inner),
        far(coupling),
    )


def leaf_kernel(
    placed_ref,
    table_ref,
    narrow_ref,
    leading_ref,
    terms_ref,
    sent_one_ref,
    kept_one_ref,
    terms_staged,
    leaving,
):
    bf16 = jnp.bfloat16
    row_count = placed_ref.shape[2]
    rank = narrow_ref.shape[1]
    split_at = row_count - rank
    slots = range(placed_ref.shape[0])
    if len(slots) == NODE_LEAVES:
        slots = [MEMBERS.index(leaf) for leaf in FIRST_MEMBERS]
    placed = jnp.concatenate([placed_ref[slot] for slot in slots], axis=0)
    basis = narrow_ref[:row_count]
    inner = narrow_ref[pl.ds(row_count, rank)]
    through = narrow_ref[pl.ds(row_count + rank, split_at)]
    one_eliminated = narrow_ref[pl.ds(row_count + rank + split_at, rank)]
    projected = product(placed, basis).astype(bf16)
    middle = product(projected, inner).astype(bf16)
    correction = product(middle, basis, ((1,), (1,)))
    reflected = (placed.astype(jnp.float32) - correction).astype(bf16)
    leading = reflected[:, :split_at]
    leading_ref[...] = leading
    coupled = product(leading, through)
    skeleton = (reflected[:, split_at:].astype(jnp.float32) - coupled).astype(bf16)
    copies = []
    share = NODE_LEAVES // leaving.shape[0]
    height = terms_staged.shape[1]
    for part in range(leaving.shape[0]):
        table = table_ref[pl.ds(part * share * height, share * height), :]
        terms = product(table, skeleton, ((1,), (1,))).astype(bf16)
        some = pl.ds(part * share, share)
        terms_staged[some] = terms.reshape((share,) + terms_staged.shape[1:])
        copies.append(
            pltpu.make_async_copy(terms_staged.at[some], terms_ref.at[some], leaving.at[part])
        )
        copies[-1].start()

    one_terms = product(skeleton, one_eliminated)
    half = rank // 2
    odd = lax.axis_index("leaf") & 1 == 1
    kept_one_ref[...] = jnp.where(odd, one_terms[:, half:], one_terms[:, :half])
    sent_one_ref[...] = jnp.where(odd, one_terms[:, :half], one_terms[:, half:]).astype(bf16)
    for copy in copies:
        copy.wait()


def leaf_stage(placed, table, narrow):
    columns = placed.shape[0] * placed.shape[1]
    rank = narrow.shape[1]
    half = rank // 2
    bf16 = jnp.bfloat16
    return pl.pallas_call(
        leaf_kernel,
        out_shape=(
            pltpu.VMEM((columns, placed.shape[2] - rank), bf16),
            pltpu.HBM((NODE_LEAVES, half, columns), bf16),
            pltpu.VMEM((columns, half), bf16),
            pltpu.VMEM((columns, half), jnp.float32),
        ),
        in_specs=[INSIDE] * 3,
        out_specs=(INSIDE, OUTSIDE, INSIDE, INSIDE),
        scratch_shapes=[
            pltpu.VMEM((NODE_LEAVES, half, columns), bf16),
            pltpu.SemaphoreType.DMA((4,)),
        ],
        compiler_params=pltpu.CompilerParams(vmem_limit_bytes=6 << 20),
    )(near(placed), near(table), near(narrow))


def eliminate_kernel(leading_ref, inverse_ref, eliminated_ref):
    eliminated_ref[...] = product(leading_ref[...], inverse_ref[...]).astype(jnp.bfloat16)


def eliminate_stage(leading, inverse):
    return pl.pallas_call(
        eliminate_kernel,
        out_shape=jax.ShapeDtypeStruct(leading.shape, jnp.bfloat16),
        in_specs=[INSIDE] * 2,
        out_specs=INSIDE,
        cost_estimate=pl.CostEstimate(
            flops=10**9, bytes_accessed=6 * 10**6, transcendentals=0
        ),
        compiler_params=pltpu.CompilerParams(vmem_limit_bytes=6 << 20),
    )(near(leading), near(inverse))


def tail_kernel(
    received_ref, received_one_ref, kept_one_ref, one_ref, two_ref, three_ref, top_ref
):
    f32 = jnp.float32
    one_ref[...] = kept_one_ref[...] + received_one_ref[...].astype(f32)
    total = jnp.sum(received_ref[...].astype(f32), axis=0)
    eighth = three_ref.shape[0]
    three_ref[...] = total[:eighth]
    top_ref[...] = total[eighth : 2 * eighth]
    two_ref[...] = total[2 * eighth :]


def tail_stage(received, received_one, kept_one):
    _, height, columns = received.shape
    shapes = [kept_one.shape] + [(height // part, columns) for part in (2, 4, 4)]
    return pl.pallas_call(
        tail_kernel,
        out_shape=[jax.ShapeDtypeStruct(shape, jnp.float32) for shape in shapes],
        in_specs=[INSIDE] * 3,
        out_specs=[INSIDE] * 4,
        compiler_params=pltpu.CompilerParams(vmem_limit_bytes=2 << 20),
    )(received, received_one, kept_one)


def shards(
    right_sides,
    block_order,
    leaf_basis,
    leaf_inner,
    leaf_inverse,
    leaf_coupling,
    merge_one,
    merge_two,
    merge_three,
):
    leaf_count = lax.axis_size("leaf")
    columns, row_count = right_sides.shape

    one_node = leaf_count == NODE_LEAVES
    first_members, members = ([list(FIRST_MEMBERS)], [list(MEMBERS)]) if one_node else (None, None)

    def spread(pieces, groups):
        return lax.all_to_all(
            pieces, "leaf", split_axis=0, concat_axis=0, tiled=True, axis_index_groups=groups
        )

    arrived = spread(right_sides.reshape(leaf_count, columns // leaf_count, row_count), first_members)

    order_kept, upper_own, three = early_stage(block_order, merge_two, merge_three)
    upper_pieces = [upper_own, exchanged(upper_own, "leaf", 1)]
    upper_pieces += [exchanged(three, "leaf", flip) for flip in (2, 3)]
    inverse, _ = lax.optimization_barrier((leaf_inverse[0], upper_own))
    inverse_far = exchanged(inverse, "rhs", 2)
    upper = jnp.concatenate(upper_pieces, axis=0)

    inverse, inverse_far, upper, _ = lax.optimization_barrier(
        (inverse, inverse_far, upper, arrived)
    )
    inverse_near = exchanged(inverse, "rhs", 1)
    inverse_last = exchanged(inverse_far, "rhs", 1)
    upper_near = exchanged(upper, "rhs", 1)
    inverse_whole, table, narrow = weights_stage(
        leaf_inverse[0],
        (inverse_far, inverse_near, inverse_last),
        upper,
        upper_near,
        merge_one,
        leaf_basis[0],
        leaf_inner[0],
        leaf_coupling[0],
    )

    if one_node:
        returning = reorder(arrived, order_kept)
    else:
        returning = reorder_anywhere(arrived, block_order)
    placed = spread(returning, members)
    leading, terms, sent_one, kept_one = leaf_stage(placed, table, narrow)

    starts = range(0, leaf_count, NODE_LEAVES)
    received = spread(terms, [[start + leaf for leaf in LAST_MEMBERS] for start in starts])
    eliminated = eliminate_stage(leading, inverse_whole)
    level_one, level_two, level_three, top_skeleton = tail_stage(
        received, exchanged(sent_one, "leaf", 1), kept_one
    )
    return (eliminated, level_one, level_two.T, level_three.T, top_skeleton.T)


def solution(mesh):
    placed = (
        P("rhs", "leaf"),
        P(),
        P("leaf", None, None),
        P("leaf", None, None),
        P("leaf", "rhs", None),
        P("leaf", None, None),
        P("leaf", None),
        P("leaf", None),
        P("leaf", None),
    )
    return jax.shard_map(
        shards,
        mesh=mesh,
        in_specs=placed,
        out_specs=(P("rhs", "leaf"),) * 5,
        check_vma=False,
    )
```

```python
import jax
import jax.numpy as jnp
from jax import lax
from jax.experimental import pallas as pl
from jax.experimental.pallas import tpu as pltpu
from jax.sharding import PartitionSpec as P

BLOCK = 128
NODE_LEAVES = 8
FIRST_MEMBERS = (4, 5, 6, 7, 0, 1, 2, 3)
MEMBERS = (4, 2, 3, 5, 0, 6, 7, 1)
LAST_MEMBERS = (5, 3, 4, 2, 1, 0, 7, 6)
INSIDE = pl.BlockSpec(memory_space=pltpu.VMEM)
SCALARS = pl.BlockSpec(memory_space=pltpu.SMEM)
OUTSIDE = pl.BlockSpec(memory_space=pl.ANY)


def near(array):
    return pltpu.with_memory_space_constraint(array, pltpu.VMEM)


def far(array):
    return pltpu.with_memory_space_constraint(array, pltpu.HBM)


def exchanged(piece, axis, flip):
    count = lax.axis_size(axis)
    return lax.ppermute(piece, axis, [(i, i ^ flip) for i in range(count) if i ^ flip < count])


def product(left, right, over=((1,), (0,))):
    return lax.dot_general(left, right, (over, ((), ())), preferred_element_type=jnp.float32)


def reorder_kernel(order_ref, rows_ref, out_ref, staged, leaving):
    per_leaf = rows_ref.shape[2] // BLOCK
    copies = []
    bits = per_leaf.bit_length() - 1
    arrived_slots = sum(slot << 3 * leaf for slot, leaf in enumerate(FIRST_MEMBERS))
    for slot, leaf in enumerate(MEMBERS):
        for t in range(per_leaf):
            source = order_ref[leaf * per_leaf + t]
            column = pl.multiple_of((source & per_leaf - 1) * BLOCK, BLOCK)
            from_slot = lax.shift_right_logical(jnp.int32(arrived_slots), (source >> bits) * 3)
            staged[slot, :, pl.ds(t * BLOCK, BLOCK)] = rows_ref[
                from_slot & 7, :, pl.ds(column, BLOCK)
            ]
        copies.append(pltpu.make_async_copy(staged.at[slot], out_ref.at[slot], leaving.at[slot]))
        copies[-1].start()
    for copy in copies:
        copy.wait()


def reorder_anywhere(rows, block_order):
    leaf_count, per_group, row_count = rows.shape
    blocks = jnp.transpose(rows.reshape(leaf_count, per_group, -1, BLOCK), (0, 2, 1, 3))
    blocks = jnp.take(blocks.reshape(-1, per_group, BLOCK), block_order, axis=0)
    blocks = blocks.reshape(leaf_count, -1, per_group, BLOCK)
    return jnp.transpose(blocks, (0, 2, 1, 3)).reshape(leaf_count, per_group, row_count)


def reorder(rows, order_kept):
    leaf_count = rows.shape[0]
    return pl.pallas_call(
        reorder_kernel,
        out_shape=pltpu.HBM(rows.shape, rows.dtype),
        in_specs=[SCALARS, INSIDE],
        out_specs=OUTSIDE,
        scratch_shapes=[
            pltpu.VMEM(rows.shape, rows.dtype),
            pltpu.SemaphoreType.DMA((leaf_count,)),
        ],
        compiler_params=pltpu.CompilerParams(vmem_limit_bytes=2 << 20),
    )(pltpu.with_memory_space_constraint(order_kept, pltpu.SMEM), near(rows))


def early_kernel(order_ref, two_ref, three_ref, order_kept_out, upper_out, three_out, arrivals):
    half = lax.axis_index("rhs") & 1
    two_half, three_half = two_ref.shape[0] // 2, three_ref.shape[0] // 2
    two = two_ref.at[pl.ds(pl.multiple_of(half * two_half, 16), two_half), :]
    three = three_ref.at[pl.ds(pl.multiple_of(half * three_half, 16), three_half), :]
    copies = [
        pltpu.make_async_copy(order_ref, order_kept_out, arrivals.at[0]),
        pltpu.make_async_copy(two, upper_out.at[pl.ds(0, two_half), :], arrivals.at[1]),
        pltpu.make_async_copy(three, upper_out.at[pl.ds(two_half, three_half), :], arrivals.at[2]),
        pltpu.make_async_copy(three, three_out, arrivals.at[3]),
    ]
    for copy in copies:
        copy.start()
    for copy in copies:
        copy.wait()


def early_stage(block_order, two, three):
    two_half, three_half, width = two.shape[0] // 2, three.shape[0] // 2, two.shape[1]
    return pl.pallas_call(
        early_kernel,
        out_shape=[
            pltpu.SMEM(block_order.shape, block_order.dtype),
            pltpu.VMEM((two_half + three_half, width), two.dtype),
            pltpu.VMEM((three_half, width), two.dtype),
        ],
        in_specs=[OUTSIDE] * 3,
        out_specs=[SCALARS] + [INSIDE] * 2,
        scratch_shapes=[pltpu.SemaphoreType.DMA((4,))],
        compiler_params=pltpu.CompilerParams(vmem_limit_bytes=1 << 20),
    )(far(block_order), far(two), far(three))


def weights_kernel(
    inverse_ref,
    inverse_far_ref,
    inverse_near_ref,
    inverse_last_ref,
    upper_ref,
    upper_near_ref,
    one_ref,
    basis_ref,
    inner_ref,
    coupling_ref,
    inverse_out,
    table_out,
    narrow_out,
    one,
    coupling,
    two_rows,
    three_rows,
    arrivals,
):
    bf16 = jnp.bfloat16
    share = lax.axis_index("rhs")
    position = lax.axis_index("leaf")
    span = inverse_ref.shape[0]
    rank = one.shape[0]
    start = pl.multiple_of(share * span, 16)
    copies = [
        pltpu.make_async_copy(one_ref, one, arrivals.at[0]),
        pltpu.make_async_copy(coupling_ref, coupling, arrivals.at[1]),
        pltpu.make_async_copy(inverse_ref, inverse_out.at[pl.ds(start, span), :], arrivals.at[2]),
    ]
    at = 0
    for index, piece in enumerate((basis_ref, inner_ref)):
        place = narrow_out.at[pl.ds(at, piece.shape[0]), :]
        copies.append(pltpu.make_async_copy(piece, place, arrivals.at[3 + index]))
        at += piece.shape[0]
    for copy in copies:
        copy.start()

    for flip, piece in ((2, inverse_far_ref), (1, inverse_near_ref), (3, inverse_last_ref)):
        start = pl.multiple_of((share ^ flip) * span, 16)
        inverse_out[pl.ds(start, span), :] = piece[...]

    two_half, three_half = rank // 4, rank // 8
    for flip, piece in ((0, upper_ref), (1, upper_near_ref)):
        half = share & 1 ^ flip
        at = 0
        for other in range(4):
            if other < 2:
                start = (position & 1 ^ other) * 2 * two_half + half * two_half
                start = pl.multiple_of(start, 16)
                two_rows[pl.ds(start, two_half), :] = piece[pl.ds(at, two_half), :]
                at += two_half
            start = (position & 3 ^ other) * 2 * three_half + half * three_half
            start = pl.multiple_of(start, 16)
            three_rows[pl.ds(start, three_half), :] = piece[pl.ds(at, three_half), :]
            at += three_half

    copies[0].wait()
    half = rank // 2
    at = narrow_out.shape[0] - rank
    narrow_out[pl.ds(at, rank), :half] = one[:, :half]
    narrow_out[pl.ds(at, rank), half:] = one[:, 2 * half : 3 * half]
    one_skeleton = jnp.concatenate([one[:, half : 2 * half], one[:, 3 * half :]], axis=1)
    through_two = product(one_skeleton, two_rows[...])
    width = rank // 4
    two_skeleton = jnp.concatenate(
        [through_two[:, (2 * g + 1) * width : (2 * g + 2) * width] for g in range(4)], axis=1
    )
    two_high = two_skeleton.astype(bf16)
    two_low = (two_skeleton - two_high.astype(jnp.float32)).astype(bf16)
    through_two = through_two.T.astype(bf16)
    three = three_rows[...]
    through_three = (product(two_high, three) + product(two_low, three)).T.astype(bf16)
    own_quad = position // 4 % 2
    for slot, leaf in enumerate(LAST_MEMBERS):
        at = 2 * slot * width
        table_out[pl.ds(at, width), :] = through_three[leaf * width : (leaf + 1) * width]
        group = leaf % 4
        two = through_two[2 * group * width : (2 * group + 1) * width]
        two = jnp.where(own_quad == leaf // 4, two, jnp.zeros_like(two))
        table_out[pl.ds(at + width, width), :] = two
    for copy in copies[1:3]:
        copy.wait()
    height = coupling.shape[0]
    at = narrow_out.shape[0] - rank - height
    narrow_out[pl.ds(at, height), :] = product(inverse_out[...], coupling[...]).astype(bf16)
    for copy in copies[3:]:
        copy.wait()


def weights_stage(inverse, inverse_pieces, upper, upper_near, one, basis, inner, coupling):
    rank = one.shape[0]
    bf16 = jnp.bfloat16
    span, extent = inverse.shape
    height = basis.shape[0] + inner.shape[0] + coupling.shape[0] + rank
    shapes = [(4 * span, extent), (4 * rank, rank), (height, rank)]
    return pl.pallas_call(
        weights_kernel,
        out_shape=[pltpu.VMEM(shape, bf16) for shape in shapes],
        in_specs=[OUTSIDE] + [INSIDE] * 5 + [OUTSIDE] * 4,
        out_specs=[INSIDE] * 3,
        scratch_shapes=[
            pltpu.VMEM((rank, 2 * rank), bf16),
            pltpu.VMEM(coupling.shape, bf16),
            pltpu.VMEM((rank, 2 * rank), bf16),
            pltpu.VMEM((rank, 2 * rank), bf16),
            pltpu.SemaphoreType.DMA((5,)),
        ],
        cost_estimate=pl.CostEstimate(
            flops=10**9, bytes_accessed=6 * 10**6, transcendentals=0
        ),
        compiler_params=pltpu.CompilerParams(vmem_limit_bytes=6 << 20),
    )(
        far(inverse),
        *map(near, inverse_pieces),
        near(upper),
        near(upper_near),
        far(one),
        far(basis),
        far(inner),
        far(coupling),
    )


def leaf_kernel(
    placed_ref,
    table_ref,
    narrow_ref,
    leading_ref,
    terms_ref,
    sent_one_ref,
    kept_one_ref,
    terms_staged,
    leaving,
):
    bf16 = jnp.bfloat16
    row_count = placed_ref.shape[2]
    rank = narrow_ref.shape[1]
    split_at = row_count - rank
    slots = range(placed_ref.shape[0])
    if len(slots) == NODE_LEAVES:
        slots = [MEMBERS.index(leaf) for leaf in FIRST_MEMBERS]
    placed = jnp.concatenate([placed_ref[slot] for slot in slots], axis=0)
    basis = narrow_ref[:row_count]
    inner = narrow_ref[pl.ds(row_count, rank)]
    through = narrow_ref[pl.ds(row_count + rank, split_at)]
    one_eliminated = narrow_ref[pl.ds(row_count + rank + split_at, rank)]
    projected = product(placed, basis).astype(bf16)
    middle = product(projected, inner).astype(bf16)
    correction = product(middle, basis, ((1,), (1,)))
    reflected = (placed.astype(jnp.float32) - correction).astype(bf16)
    leading = reflected[:, :split_at]
    leading_ref[...] = leading
    coupled = product(leading, through)
    skeleton = (reflected[:, split_at:].astype(jnp.float32) - coupled).astype(bf16)
    copies = []
    share = NODE_LEAVES // leaving.shape[0]
    height = terms_staged.shape[1]
    for part in range(leaving.shape[0]):
        table = table_ref[pl.ds(part * share * height, share * height), :]
        terms = product(table, skeleton, ((1,), (1,))).astype(bf16)
        some = pl.ds(part * share, share)
        terms_staged[some] = terms.reshape((share,) + terms_staged.shape[1:])
        copies.append(
            pltpu.make_async_copy(terms_staged.at[some], terms_ref.at[some], leaving.at[part])
        )
        copies[-1].start()

    one_terms = product(skeleton, one_eliminated)
    half = rank // 2
    odd = lax.axis_index("leaf") & 1 == 1
    kept_one_ref[...] = jnp.where(odd, one_terms[:, half:], one_terms[:, :half])
    sent_one_ref[...] = jnp.where(odd, one_terms[:, :half], one_terms[:, half:]).astype(bf16)
    for copy in copies:
        copy.wait()


def leaf_stage(placed, table, narrow):
    columns = placed.shape[0] * placed.shape[1]
    rank = narrow.shape[1]
    half = rank // 2
    bf16 = jnp.bfloat16
    return pl.pallas_call(
        leaf_kernel,
        out_shape=(
            pltpu.VMEM((columns, placed.shape[2] - rank), bf16),
            pltpu.HBM((NODE_LEAVES, half, columns), bf16),
            pltpu.VMEM((columns, half), bf16),
            pltpu.VMEM((columns, half), jnp.float32),
        ),
        in_specs=[INSIDE] * 3,
        out_specs=(INSIDE, OUTSIDE, INSIDE, INSIDE),
        scratch_shapes=[
            pltpu.VMEM((NODE_LEAVES, half, columns), bf16),
            pltpu.SemaphoreType.DMA((4,)),
        ],
        compiler_params=pltpu.CompilerParams(vmem_limit_bytes=6 << 20),
    )(near(placed), near(table), near(narrow))


def eliminate_kernel(leading_ref, inverse_ref, eliminated_ref):
    eliminated_ref[...] = product(leading_ref[...], inverse_ref[...]).astype(jnp.bfloat16)


def eliminate_stage(leading, inverse):
    return pl.pallas_call(
        eliminate_kernel,
        out_shape=jax.ShapeDtypeStruct(leading.shape, jnp.bfloat16),
        in_specs=[INSIDE] * 2,
        out_specs=INSIDE,
        cost_estimate=pl.CostEstimate(
            flops=10**9, bytes_accessed=6 * 10**6, transcendentals=0
        ),
        compiler_params=pltpu.CompilerParams(vmem_limit_bytes=6 << 20),
    )(near(leading), near(inverse))


def tail_kernel(
    received_ref, received_one_ref, kept_one_ref, one_ref, two_ref, three_ref, top_ref
):
    f32 = jnp.float32
    one_ref[...] = kept_one_ref[...] + received_one_ref[...].astype(f32)
    total = jnp.sum(received_ref[...].astype(f32), axis=0)
    eighth = three_ref.shape[0]
    three_ref[...] = total[:eighth]
    top_ref[...] = total[eighth : 2 * eighth]
    two_ref[...] = total[2 * eighth :]


def tail_stage(received, received_one, kept_one):
    _, height, columns = received.shape
    shapes = [kept_one.shape] + [(height // part, columns) for part in (2, 4, 4)]
    return pl.pallas_call(
        tail_kernel,
        out_shape=[jax.ShapeDtypeStruct(shape, jnp.float32) for shape in shapes],
        in_specs=[INSIDE] * 3,
        out_specs=[INSIDE] * 4,
        compiler_params=pltpu.CompilerParams(vmem_limit_bytes=2 << 20),
    )(received, received_one, kept_one)


def shards(
    right_sides,
    block_order,
    leaf_basis,
    leaf_inner,
    leaf_inverse,
    leaf_coupling,
    merge_one,
    merge_two,
    merge_three,
):
    leaf_count = lax.axis_size("leaf")
    columns, row_count = right_sides.shape

    one_node = leaf_count == NODE_LEAVES
    first_members, members = ([list(FIRST_MEMBERS)], [list(MEMBERS)]) if one_node else (None, None)

    def spread(pieces, groups):
        return lax.all_to_all(
            pieces, "leaf", split_axis=0, concat_axis=0, tiled=True, axis_index_groups=groups
        )

    arrived = spread(right_sides.reshape(leaf_count, columns // leaf_count, row_count), first_members)

    order_kept, upper_own, three = early_stage(block_order, merge_two, merge_three)
    upper_pieces = [upper_own, exchanged(upper_own, "leaf", 1)]
    upper_pieces += [exchanged(three, "leaf", flip) for flip in (2, 3)]
    inverse, _ = lax.optimization_barrier((leaf_inverse[0], upper_own))
    inverse_far = exchanged(inverse, "rhs", 2)
    upper = jnp.concatenate(upper_pieces, axis=0)

    inverse, inverse_far, upper, _ = lax.optimization_barrier(
        (inverse, inverse_far, upper, arrived)
    )
    inverse_near = exchanged(inverse, "rhs", 1)
    inverse_last = exchanged(inverse_far, "rhs", 1)
    upper_near = exchanged(upper, "rhs", 1)
    inverse_whole, table, narrow = weights_stage(
        leaf_inverse[0],
        (inverse_far, inverse_near, inverse_last),
        upper,
        upper_near,
        merge_one,
        leaf_basis[0],
        leaf_inner[0],
        leaf_coupling[0],
    )

    if one_node:
        returning = reorder(arrived, order_kept)
    else:
        returning = reorder_anywhere(arrived, block_order)
    placed = spread(returning, members)
    leading, terms, sent_one, kept_one = leaf_stage(placed, table, narrow)

    starts = range(0, leaf_count, NODE_LEAVES)
    received = spread(terms, [[start + leaf for leaf in LAST_MEMBERS] for start in starts])
    eliminated = eliminate_stage(leading, inverse_whole)
    level_one, level_two, level_three, top_skeleton = tail_stage(
        received, exchanged(sent_one, "leaf", 1), kept_one
    )
    return (eliminated, level_one, level_two.T, level_three.T, top_skeleton.T)


def solution(mesh):
    placed = (
        P("rhs", "leaf"),
        P(),
        P("leaf", None, None),
        P("leaf", None, None),
        P("leaf", "rhs", None),
        P("leaf", None, None),
        P("leaf", None),
        P("leaf", None),
        P("leaf", None),
    )
    return jax.shard_map(
        shards,
        mesh=mesh,
        in_specs=placed,
        out_specs=(P("rhs", "leaf"),) * 5,
        check_vma=False,
    )
```
